32 devices in a mesh: dp: 8 (over z, y), seq: 4 (over x, core).
Axes of the slice: x: 2, y: 2, z: 4, core: 2. Of those that a mesh axis runs over, the one named last changes fastest.
Arguments:
- sequence_in: bfloat16 [8, 2048, 768], P('dp', 'seq'), may hold values from -6 to 6
- output_grad: bfloat16 [8, 2048, 768], P('dp', 'seq'), may hold values from -6 to 6
- skip_mask: int32 [8, 2], P('dp'), may hold values 0 or 1
- in_gain: float32 [2, 768], replicated, may hold values from 0.25 to 1.75
- input_shift_vec: float32 [2, 768], replicated, may hold values from -3 to 3
- mid_gain: float32 [2, 384], replicated, may hold values from 0.25 to 1.75
- mid_offset: float32 [2, 384], replicated, may hold values from -3 to 3
- conv_weight: bfloat16 [2, 3, 768, 384], P(None, None, 'seq'), may hold values from -0.21875 to 0.21875
- point_weight: bfloat16 [384, 2, 768], P('seq'), may hold values from -0.3125 to 0.3125
Outputs:
- point_grad: float32 [384, 2, 768], P('seq')
- input_grad: bfloat16 [8, 2048, 768], P('dp', 'seq')
The draws below stay inside these ranges and needn't reach their ends.
Inputs may be any that keep to these rules, and one draw needn't show every extreme that they name: skip_mask[s, b] = 1 means that sample s passes block b unchanged in this step.
All inputs are finite; a program needn't handle non-finite values.
Results may differ from the reference program's by a relative error of at most 0.009.
Values may be sent and summed in bfloat16 or wider, within the bound.
A program may use at most 64 MiB of HBM per device.

```python
import math
import jax
import jax.numpy as jnp
from jax import lax

C = 768
H = 384
FIRST_DILATION = 1024
SECOND_DILATION = 2048
SAMPLES = 8
LENGTH = 2048


def touch_ends(array, stream_key, smallest, largest):
    longest = array.shape.index(max(array.shape))
    spots = []
    for shift in (0, 1):
        where = [jax.random.randint(jax.random.fold_in(stream_key, axis), (), 0, length) for axis, length in enumerate(array.shape)]
        where[longest] = (where[longest] + shift) % array.shape[longest]
        spots.append(tuple(where))
    return array.at[spots[0]].set(smallest).at[spots[1]].set(largest)


def level_of(key, dims, shards, least, high):
    loudness, own = 1.0, jax.random.fold_in(key, 6)
    for position, blocks in shards:
        draws = jnp.exp(jax.random.uniform(jax.random.fold_in(own, position), (blocks,), jnp.float32, least / len(shards), high / len(shards)))
        loudness = loudness * jnp.repeat(draws, dims[position] // blocks).reshape([-1 if axis == position else 1 for axis in range(len(dims))])
    return loudness


def noise(stream_key, dims, width, reach, cuts=(), held_as=jnp.bfloat16):
    result = width * jax.random.normal(stream_key, dims, jnp.float32)
    if cuts:
        result = result * level_of(stream_key, dims, cuts, -0.22, 0.18)
    return jnp.clip(result, -reach, reach).astype(held_as)


def setup_inputs(seed: int = 0) -> dict:
    arg_keys = jax.random.split(jax.random.key(seed), 10)
    return {
        "sequence_in": noise(arg_keys[0], (SAMPLES, LENGTH, C), 1.0, 6.0, ((0, 8), (1, 4))),
        "output_grad": noise(arg_keys[1], (SAMPLES, LENGTH, C), 1.0, 6.0, ((0, 8), (1, 4))),
        "skip_mask": touch_ends((jax.random.randint(arg_keys[2], (SAMPLES, 2), 0, 4) < 1).astype(jnp.int32), jax.random.fold_in(arg_keys[2], 1), 0, 1),
        "in_gain": jnp.clip(1.0 + 0.15 * jax.random.normal(arg_keys[3], (2, C), jnp.float32), 0.25, 1.75),
        "input_shift_vec": noise(arg_keys[4], (2, C), 0.5, 3.0, (), jnp.float32),
        "mid_gain": jnp.clip(1.0 + 0.15 * jax.random.normal(arg_keys[5], (2, H), jnp.float32), 0.25, 1.75),
        "mid_offset": noise(arg_keys[6], (2, H), 0.5, 3.0, (), jnp.float32),
        "conv_weight": noise(arg_keys[7], (2, 3, C, H), C ** -0.5, 0.21875, ((2, 4),)),
        "point_weight": noise(arg_keys[8], (H, 2, C), H ** -0.5, 0.3125, ((0, 4),)),
    }


def gelu_tanh(values):
    return jax.nn.gelu(values, approximate=True)

def dilated_taps(source, distance):
    length = source.shape[0]
    if distance >= length:
        return (jnp.zeros_like(source), jnp.zeros_like(source))
    padding = jnp.zeros((distance, source.shape[1]), source.dtype)
    earlier = jnp.concatenate([padding, source[:length - distance]], axis=0)
    later = jnp.concatenate([source[distance:], padding], axis=0)
    return (earlier, later)

def contract_last(left, right):
    return lax.dot_general(left, right, (((1,), (1,)), ((), ())), preferred_element_type=jnp.float32)

def reference(sequence_in, output_grad, skip_mask, in_gain, input_shift_vec, mid_gain, mid_offset, conv_weight, point_weight):
    dilation_list = (FIRST_DILATION, SECOND_DILATION)

    def single_sample(carry, inputs):
        sample_in, sample_grad, sample_skip = inputs
        state = sample_in
        stored = []
        for block_index in range(2):
            kept_flag = (1 - sample_skip[block_index]).astype(jnp.float32)
            normed = state.astype(jnp.float32) * in_gain[block_index] + input_shift_vec[block_index]
            activated = gelu_tanh(normed).astype(jnp.bfloat16)
            earlier, later = dilated_taps(activated, dilation_list[block_index])
            weight = conv_weight[block_index]
            conv_out = jnp.dot(earlier, weight[0], preferred_element_type=jnp.float32)
            conv_out = conv_out + jnp.dot(activated, weight[1], preferred_element_type=jnp.float32)
            conv_out = conv_out + jnp.dot(later, weight[2], preferred_element_type=jnp.float32)
            middle = conv_out * mid_gain[block_index] + mid_offset[block_index]
            hidden_act = gelu_tanh(middle).astype(jnp.bfloat16)
            branch = jnp.dot(hidden_act, point_weight[:, block_index, :], preferred_element_type=jnp.float32)
            stored.append((normed, middle, hidden_act, kept_flag))
            state = (state.astype(jnp.float32) + kept_flag * branch).astype(jnp.bfloat16)
        gradient = sample_grad
        terms = [None, None]
        for block_index in (1, 0):
            normed, middle, hidden_act, kept_flag = stored[block_index]
            branch_grad = (kept_flag * gradient.astype(jnp.float32)).astype(jnp.bfloat16)
            terms[block_index] = lax.dot_general(hidden_act, branch_grad, (((0,), (0,)), ((), ())), preferred_element_type=jnp.float32)
            hidden_grad = contract_last(branch_grad, point_weight[:, block_index, :])
            middle_grad = jax.vjp(gelu_tanh, middle)[1](hidden_grad)[0]
            conv_grad = (middle_grad * mid_gain[block_index]).astype(jnp.bfloat16)
            earlier, later = dilated_taps(conv_grad, dilation_list[block_index])
            weight = conv_weight[block_index]
            act_grad = contract_last(later, weight[0]) + contract_last(conv_grad, weight[1]) + contract_last(earlier, weight[2])
            normed_grad = jax.vjp(gelu_tanh, normed)[1](act_grad)[0] * in_gain[block_index]
            gradient = (gradient.astype(jnp.float32) + normed_grad).astype(jnp.bfloat16)
        return (carry + jnp.stack(terms, axis=1), gradient)
    start_sum = jnp.zeros((H, 2, C), jnp.float32)
    summed, input_grad = lax.scan(single_sample, start_sum, (sequence_in, output_grad, skip_mask))
    point_grad = summed * (1.0 / math.sqrt(SAMPLES * LENGTH))
    return (point_grad, input_grad)
```

```python
import functools
import math

import jax
import jax.numpy as jnp
from jax import lax
from jax.experimental import pallas as pl
from jax.experimental.pallas import tpu as pltpu
from jax.sharding import PartitionSpec as P

FIRST_DILATION = 1024
SECOND_DILATION = 2048


def passed_along(value, axis, by):
    peers = lax.axis_size(axis)
    pairs = [(i, i + by) for i in range(peers) if 0 <= i + by < peers]
    return lax.ppermute(value, axis, pairs)


def gelu_tanh(values):
    return jax.nn.gelu(values, approximate=True)


def contract_last(left, right):
    return lax.dot_general(
        left, right, (((1,), (1,)), ((), ())), preferred_element_type=jnp.float32
    )


def neighbours(source, shards_away):
    if shards_away >= lax.axis_size("seq"):
        return (jnp.zeros_like(source), jnp.zeros_like(source))
    earlier = passed_along(source, "seq", shards_away)
    later = passed_along(source, "seq", -shards_away)
    return (earlier, later)


def forward_local(
    state, earlier, activated, later, weight, gain_vec, offset_vec, projection, kept_flag
):
    conv_out = jnp.dot(earlier, weight[0], preferred_element_type=jnp.float32)
    conv_out = conv_out + jnp.dot(activated, weight[1], preferred_element_type=jnp.float32)
    conv_out = conv_out + jnp.dot(later, weight[2], preferred_element_type=jnp.float32)
    middle = conv_out * gain_vec + offset_vec
    hidden_act = gelu_tanh(middle).astype(jnp.bfloat16)
    branch = jnp.dot(hidden_act, projection, preferred_element_type=jnp.float32)
    result = (state.astype(jnp.float32) + kept_flag * branch).astype(jnp.bfloat16)
    return (middle, hidden_act, result)


def backward_first(gradient, middle, projection, gain_vec, kept_flag):
    branch_grad = (kept_flag * gradient.astype(jnp.float32)).astype(jnp.bfloat16)
    hidden_grad = contract_last(branch_grad, projection)
    middle_grad = jax.vjp(gelu_tanh, middle)[1](hidden_grad)[0]
    conv_grad = (middle_grad * gain_vec).astype(jnp.bfloat16)
    return (conv_grad, branch_grad)


def backward_second(gradient, earlier, conv_grad, later, weight, normed, gain_vec):
    act_grad = (
        contract_last(later, weight[0])
        + contract_last(conv_grad, weight[1])
        + contract_last(earlier, weight[2])
    )
    normed_grad = jax.vjp(gelu_tanh, normed)[1](act_grad)[0] * gain_vec
    return (gradient.astype(jnp.float32) + normed_grad).astype(jnp.bfloat16)


def grad_rows(hidden_act, branch_grad):
    return lax.dot_general(
        hidden_act, branch_grad, (((0,), (0,)), ((), ())), preferred_element_type=jnp.float32
    )


MESH = pl.DeviceIdType.MESH
CHUNKS = 4
PIECES = 5
TANH_SCALE = 0.7978845608028654
CUBIC = 0.044715


def gelu_and_slope(values):
    squared = values * values
    tanh = jnp.tanh(values * (TANH_SCALE + (TANH_SCALE * CUBIC) * squared))
    gate = 0.5 + 0.5 * tanh
    bend = values * (0.5 - 0.5 * tanh * tanh)
    slope = gate + bend * (TANH_SCALE + (3.0 * TANH_SCALE * CUBIC) * squared)
    return values * gate, slope


def gelu_only(values):
    tanh = jnp.tanh(values * (TANH_SCALE + (TANH_SCALE * CUBIC) * (values * values)))
    return values * (0.5 + 0.5 * tanh)


def dot(left, right):
    return jnp.dot(left, right, preferred_element_type=jnp.float32)


def paired_kernel(
    x_ref,
    og_ref,
    skip_ref,
    in_gain_ref,
    in_shift_ref,
    mid_gain_ref,
    mid_offset_ref,
    cw_ref,
    pw_ref,
    pg_ref,
    gin_ref,
    wbuf,
    wpoint,
    act0,
    slope0,
    own_conv,
    hidden_grad1,
    part_out,
    part_in,
    cgrad_out,
    cgrad_in,
    hidden0,
    hidden1,
    bgrad0,
    bgrad1,
    grad1,
    term,
    term_out,
    core_in,
    x_out,
    x_in,
    summed,
    y_out,
    y_in,
    z_keep,
    z_out,
    z_in,
    final,
    ssem,
    rsem,
):
    seq = lax.axis_index("seq")
    dp = lax.axis_index("dp")
    core = seq % 2
    xpos = seq // 2
    ypos = dp % 2
    zpos = dp // 2
    depth = z_in.shape[0]
    core_mate = {"seq": seq + 1 - 2 * core}
    x_mate = {"seq": (seq + 2) % 4}
    y_mate = {"dp": dp + 1 - 2 * ypos}
    z_mates = [{"dp": (dp + 2 * j) % (2 * depth)} for j in range(1, depth)]
    rows = x_ref.shape[0]
    size = rows // CHUNKS
    channels = x_ref.shape[1]
    hidden = own_conv.shape[1]
    tap = 2 * xpos

    barrier = pltpu.get_barrier_semaphore()
    peers = [core_mate, x_mate, y_mate] + z_mates
    for peer in peers:
        pl.semaphore_signal(barrier, inc=1, device_id=peer, device_id_type=MESH)
    pl.semaphore_wait(barrier, len(peers))

    def remote(src, dst, index, peer):
        return pltpu.make_async_remote_copy(
            src_ref=src,
            dst_ref=dst,
            send_sem=ssem.at[index],
            recv_sem=rsem.at[index],
            device_id=peer,
            device_id_type=MESH,
        )

    def mine(piece, for_mate):
        if piece == 0:
            return cw_ref.at[0, 2 - tap if for_mate else tap]
        return (None, cw_ref.at[0, 1], pw_ref.at[0], cw_ref.at[1, 1], pw_ref.at[1])[piece]

    def place(piece, owner):
        where = (wbuf.at[0], wbuf.at[1], wpoint.at[0], wbuf.at[2], wpoint.at[1])[piece]
        return where.at[owner]

    far = (seq + 2) % 4
    to_core, to_x, to_y, fwd_x, fwd_y = [], [], [], [], []
    for k in range(PIECES):
        to_core.append(remote(mine(k, False), place(k, seq), 5 * k, core_mate))
        to_x.append(
            remote(mine(k, True).at[ypos], place(k, seq).at[ypos], 5 * k + 1, x_mate)
        )
        half = place(k, far).at[ypos]
        to_y.append(remote(half, half, 5 * k + 2, y_mate))
        fwd_x.append(remote(half, half, 5 * k + 3, core_mate))
        other = place(k, far).at[1 - ypos]
        fwd_y.append(remote(other, other, 5 * k + 4, core_mate))
    for k in range(PIECES):
        to_x[k].start()
        to_core[k].start()

    def after_x(k):
        to_x[k].wait_recv()
        to_y[k].start()
        fwd_x[k].start()

    def after_y(k):
        to_y[k].wait_recv()
        fwd_y[k].start()

    def ready(k):
        to_core[k].wait_recv()
        fwd_x[k].wait_recv()
        fwd_y[k].wait_recv()

    for k in range(PIECES):
        place(k, seq)[...] = mine(k, False)[...]

    keep = [(1 - skip_ref[0, b]).astype(jnp.float32) for b in range(2)]
    in_gain = [in_gain_ref[b : b + 1, :] for b in range(2)]
    in_shift = [in_shift_ref[b : b + 1, :] for b in range(2)]
    mid_gain = [mid_gain_ref[b : b + 1, :] for b in range(2)]
    mid_offset = [mid_offset_ref[b : b + 1, :] for b in range(2)]

    def conv_full(k):
        return wbuf[k].reshape(channels, hidden)

    def point_full(b):
        return wpoint[b].reshape(hidden, channels)

    def at(r):
        return pl.ds(pl.multiple_of(r * size, size), size)

    def chunked(body):
        def step(r, carry):
            body(r)
            return carry

        lax.fori_loop(0, CHUNKS, step, 0)

    def start_block(r):
        spot = at(r)
        value = x_ref[spot, :].astype(jnp.float32) * in_gain[0] + in_shift[0]
        gelu, slope = gelu_and_slope(value)
        act0[spot, :] = gelu.astype(jnp.bfloat16)
        slope0[spot, :] = slope * in_gain[0]
        bgrad1[spot, :] = (keep[1] * og_ref[spot, :].astype(jnp.float32)).astype(jnp.bfloat16)

    chunked(start_block)

    part_base = 5 * PIECES
    cgrad_base = part_base + CHUNKS
    term_base = cgrad_base + CHUNKS

    def part_copy(r):
        return remote(part_out.at[at(r)], part_in.at[at(r)], part_base + r, x_mate)

    def cgrad_copy(r):
        return remote(cgrad_out.at[at(r)], cgrad_in.at[at(r)], cgrad_base + r, x_mate)

    after_x(0)
    after_x(1)
    after_y(0)
    ready(0)

    def make_part(r):
        spot = at(r)
        part_out[spot, :] = dot(act0[spot, :], conv_full(0)).astype(jnp.bfloat16)
        part_copy(r).start()

    chunked(make_part)
    after_x(2)
    after_y(1)
    after_x(3)
    after_y(2)
    ready(1)

    def make_own(r):
        spot = at(r)
        own_conv[spot, :] = dot(act0[spot, :], conv_full(1))

    chunked(make_own)
    after_x(4)
    after_y(3)
    after_y(4)
    ready(4)

    def make_hidden_grad(r):
        spot = at(r)
        hidden_grad1[spot, :] = contract_last(bgrad1[spot, :], point_full(1))

    chunked(make_hidden_grad)
    ready(2)
    ready(3)

    def middle_part(r):
        spot = at(r)
        part_copy(r).wait_recv()
        conv = own_conv[spot, :] + part_in[spot, :].astype(jnp.float32)
        gelu, mid_slope0 = gelu_and_slope(conv * mid_gain[0] + mid_offset[0])
        act_hidden0 = gelu.astype(jnp.bfloat16)
        hidden0[spot, :] = act_hidden0
        branch = dot(act_hidden0, point_full(0))
        state = (x_ref[spot, :].astype(jnp.float32) + keep[0] * branch).astype(jnp.bfloat16)
        gelu, slope1 = gelu_and_slope(state.astype(jnp.float32) * in_gain[1] + in_shift[1])
        conv = dot(gelu.astype(jnp.bfloat16), conv_full(2))
        gelu, mid_slope1 = gelu_and_slope(conv * mid_gain[1] + mid_offset[1])
        hidden1[spot, :] = gelu.astype(jnp.bfloat16)
        conv_grad = (mid_slope1 * hidden_grad1[spot, :] * mid_gain[1]).astype(jnp.bfloat16)
        act_grad = contract_last(conv_grad, conv_full(2))
        gradient = (
            og_ref[spot, :].astype(jnp.float32) + slope1 * act_grad * in_gain[1]
        ).astype(jnp.bfloat16)
        grad1[spot, :] = gradient
        branch_grad = (keep[0] * gradient.astype(jnp.float32)).astype(jnp.bfloat16)
        bgrad0[spot, :] = branch_grad
        hidden_grad = contract_last(branch_grad, point_full(0))
        cgrad_out[spot, :] = (mid_slope0 * hidden_grad * mid_gain[0]).astype(jnp.bfloat16)
        cgrad_copy(r).start()

    chunked(middle_part)

    core_copy = [
        remote(term_out.at[b, 1 - core], core_in.at[b], term_base + b, core_mate)
        for b in range(2)
    ]
    x_copy = [remote(x_out.at[b], x_in.at[b], term_base + 2 + b, x_mate) for b in range(2)]
    y_copy = remote(y_out, y_in, term_base + 4, y_mate)
    z_copy = [
        remote(z_out.at[(zpos + j) % depth], z_in.at[j], term_base + 4 + j, z_mates[j - 1])
        for j in range(1, depth)
    ]
    gather_base = term_base + 4 + depth
    own_quarter = final.at[ypos, zpos]
    z_gather = [
        remote(own_quarter, own_quarter, gather_base + j - 1, z_mates[j - 1])
        for j in range(1, depth)
    ]
    y_gather = []
    for j in range(depth):
        quarter = final.at[ypos, (zpos + depth - j) % depth]
        y_gather.append(remote(quarter, quarter, gather_base + depth - 1 + j, y_mate))

    share = hidden // 4
    for b, kept, branch in ((1, hidden1, bgrad1), (0, hidden0, bgrad0)):
        product = grad_rows(kept[...], branch[...])
        for owner in range(4):
            block = product[owner * share : (owner + 1) * share, :]
            term[b, owner % 2, owner // 2] = block
            term_out[b, owner % 2, owner // 2] = block.astype(jnp.bfloat16)
        core_copy[b].start()

    def last_part(r):
        spot = at(r)
        cgrad_copy(r).wait_recv()
        act_grad = contract_last(cgrad_out[spot, :], conv_full(1))
        act_grad = act_grad + contract_last(cgrad_in[spot, :], conv_full(0))
        gin_ref[spot, :] = (
            grad1[spot, :].astype(jnp.float32) + slope0[spot, :] * act_grad
        ).astype(jnp.bfloat16)

    for b in (1, 0):
        core_copy[b].wait_recv()
        away = term[b, core, 1 - xpos] + core_in[b, 1 - xpos].astype(jnp.float32)
        x_out[b] = away.astype(jnp.bfloat16)
        x_copy[b].start()
    last_part(0)
    for b in (1, 0):
        near = term[b, core, xpos] + core_in[b, xpos].astype(jnp.float32)
        x_copy[b].wait_recv()
        summed[b] = near + x_in[b].astype(jnp.float32)
    y_out[...] = summed[1 - ypos].astype(jnp.bfloat16)
    y_copy.start()
    last_part(1)
    y_copy.wait_recv()
    half_rows, half_cols = z_keep.shape[1:]
    whole = summed[ypos] + y_in[...].astype(jnp.float32)
    for q in range(depth):
        row, col = (q // 2) * half_rows, (q % 2) * half_cols
        block = whole[row : row + half_rows, col : col + half_cols]
        z_keep[q] = block
        z_out[q] = block.astype(jnp.bfloat16)
    for copy in z_copy:
        copy.start()
    last_part(2)
    total = z_keep[zpos]
    for j in range(1, depth):
        z_copy[j - 1].wait_recv()
        total = total + z_in[j].astype(jnp.float32)
    final[ypos, zpos] = total.astype(jnp.bfloat16)
    for copy in z_gather:
        copy.start()
    y_gather[0].start()
    last_part(3)
    for j in range(1, depth):
        z_gather[j - 1].wait_recv()
        y_gather[j].start()
    for copy in y_gather:
        copy.wait_recv()
    for b in range(2):
        for q in range(depth):
            row, col = (q // 2) * half_rows, (q % 2) * half_cols
            pg_ref[b, row : row + half_rows, col : col + half_cols] = final[b, q]

    for group in (to_core, to_x, to_y, fwd_x, fwd_y, core_copy, x_copy, z_copy, z_gather, y_gather):
        for copy in group:
            copy.wait_send()
    y_copy.wait_send()
    for r in range(CHUNKS):
        part_copy(r).wait_send()
        cgrad_copy(r).wait_send()


def paired_shards(
    sequence_in,
    output_grad,
    skip_mask,
    in_gain,
    input_shift_vec,
    mid_gain,
    mid_offset,
    conv_weight,
    point_weight,
):
    rows, channels = sequence_in.shape[1:]
    hidden = conv_weight.shape[3]
    share = point_weight.shape[0]
    depth = lax.axis_size("dp") // 2
    taps = conv_weight.reshape(2, 3, 2, -1, hidden)
    points = jnp.transpose(point_weight, (1, 0, 2)).reshape(2, 2, -1, channels)
    taps_shape = taps.shape[2:]
    points_shape = points.shape[1:]
    copies = 5 * PIECES + 2 * CHUNKS + 5 + 3 * depth
    vmem = pl.BlockSpec(memory_space=pltpu.VMEM)
    bf16, f32 = jnp.bfloat16, jnp.float32
    quarter = (share // 2, channels // 2)
    scratch = [
        pltpu.VMEM((3, 4) + taps_shape, bf16),
        pltpu.VMEM((2, 4) + points_shape, bf16),
        pltpu.VMEM((rows, channels), bf16),
        pltpu.VMEM((rows, channels), f32),
        pltpu.VMEM((rows, hidden), f32),
        pltpu.VMEM((rows, hidden), f32),
        pltpu.VMEM((rows, hidden), bf16),
        pltpu.VMEM((rows, hidden), bf16),
        pltpu.VMEM((rows, hidden), bf16),
        pltpu.VMEM((rows, hidden), bf16),
        pltpu.VMEM((rows, hidden), bf16),
        pltpu.VMEM((rows, hidden), bf16),
        pltpu.VMEM((rows, channels), bf16),
        pltpu.VMEM((rows, channels), bf16),
        pltpu.VMEM((rows, channels), bf16),
        pltpu.VMEM((2, 2, 2, share, channels), f32),
        pltpu.VMEM((2, 2, 2, share, channels), bf16),
        pltpu.VMEM((2, 2, share, channels), bf16),
        pltpu.VMEM((2, share, channels), bf16),
        pltpu.VMEM((2, share, channels), bf16),
        pltpu.VMEM((2, share, channels), f32),
        pltpu.VMEM((share, channels), bf16),
        pltpu.VMEM((share, channels), bf16),
        pltpu.VMEM((depth,) + quarter, f32),
        pltpu.VMEM((depth,) + quarter, bf16),
        pltpu.VMEM((depth,) + quarter, bf16),
        pltpu.VMEM((2, depth) + quarter, bf16),
        pltpu.SemaphoreType.DMA((copies,)),
        pltpu.SemaphoreType.DMA((copies,)),
    ]
    summed, gradient = pl.pallas_call(
        paired_kernel,
        out_shape=(
            jax.ShapeDtypeStruct((2, share, channels), bf16),
            jax.ShapeDtypeStruct((rows, channels), bf16),
        ),
        in_specs=[vmem, vmem, pl.BlockSpec(memory_space=pltpu.SMEM)] + [vmem] * 6,
        out_specs=(vmem, vmem),
        scratch_shapes=scratch,
        compiler_params=pltpu.CompilerParams(
            collective_id=0, has_side_effects=True, vmem_limit_bytes=48 * 2**20
        ),
    )(
        sequence_in.reshape(rows, channels),
        output_grad.reshape(rows, channels),
        skip_mask,
        in_gain,
        input_shift_vec,
        mid_gain,
        mid_offset,
        taps,
        points,
    )
    sample_count = sequence_in.shape[0] * lax.axis_size("dp")
    full_length = rows * lax.axis_size("seq")
    scale = 1.0 / math.sqrt(sample_count * full_length)
    point_grad = jnp.transpose(summed, (1, 0, 2)).astype(f32) * scale
    return (point_grad, gradient.reshape(sequence_in.shape))


def pairs_apply(sequence_in):
    count, positions = sequence_in.shape[:2]
    peers = lax.axis_size("seq")
    reach = (FIRST_DILATION // positions, SECOND_DILATION // positions)
    return (
        count == 1
        and peers == 4
        and lax.axis_size("dp") == 8
        and 2 * reach[0] == peers
        and reach[1] >= peers
    )


def shards(
    sequence_in,
    output_grad,
    skip_mask,
    in_gain,
    input_shift_vec,
    mid_gain,
    mid_offset,
    conv_weight,
    point_weight,
):
    if pairs_apply(sequence_in):
        return paired_shards(
            sequence_in,
            output_grad,
            skip_mask,
            in_gain,
            input_shift_vec,
            mid_gain,
            mid_offset,
            conv_weight,
            point_weight,
        )
    position_list = sequence_in.shape[1]
    channels = sequence_in.shape[2]
    point_full = lax.all_gather(point_weight, "seq", axis=0, tiled=True)
    neighbour_reach = (FIRST_DILATION // position_list, SECOND_DILATION // position_list)
    state = sequence_in.reshape(-1, channels)
    total_rows = state.shape[0]
    saved = []
    kept_weights = []
    for block_index in range(2):
        kept_flag = (1 - skip_mask[0, block_index]).astype(jnp.float32)
        normed = state.astype(jnp.float32) * in_gain[block_index] + input_shift_vec[block_index]
        activated = gelu_tanh(normed).astype(jnp.bfloat16)
        earlier, later = neighbours(
            activated.reshape(sequence_in.shape), neighbour_reach[block_index]
        )
        earlier = earlier.reshape(total_rows, channels)
        later = later.reshape(total_rows, channels)
        weight = lax.all_gather(conv_weight[block_index], "seq", axis=1, tiled=True)
        kept_weights.append(weight)
        operands = (
            state,
            earlier,
            activated,
            later,
            weight,
            mid_gain[block_index],
            mid_offset[block_index],
            point_full[:, block_index, :],
            kept_flag,
        )
        middle, hidden_act, state = forward_local(*operands)
        saved.append((normed, middle, hidden_act, kept_flag))
    gradient = output_grad.reshape(-1, channels)
    hidden_saved = [None, None]
    branch_saved = [None, None]
    for block_index in (1, 0):
        normed, middle, hidden_act, kept_flag = saved[block_index]
        projection = point_full[:, block_index, :]
        first_operands = (gradient, middle, projection, mid_gain[block_index], kept_flag)
        conv_grad, branch_grad = backward_first(*first_operands)
        hidden_saved[block_index] = hidden_act
        branch_saved[block_index] = branch_grad
        earlier, later = neighbours(
            conv_grad.reshape(sequence_in.shape[0], position_list, -1), neighbour_reach[block_index]
        )
        earlier = earlier.reshape(total_rows, -1)
        later = later.reshape(total_rows, -1)
        weight = lax.all_gather(conv_weight[block_index], "seq", axis=1, tiled=True)
        second_operands = (
            gradient,
            earlier,
            conv_grad,
            later,
            weight,
            normed,
            in_gain[block_index],
        )
        gradient = backward_second(*second_operands)
    first_term = grad_rows(hidden_saved[0], branch_saved[0])
    second_term = grad_rows(hidden_saved[1], branch_saved[1])
    shared_part = lax.psum_scatter(
        jnp.stack([first_term, second_term], axis=1), "seq", scatter_dimension=0, tiled=True
    )
    summed = lax.psum(shared_part, "dp")
    sample_count = sequence_in.shape[0] * lax.axis_size("dp")
    full_length = position_list * lax.axis_size("seq")
    point_grad = summed * (1.0 / math.sqrt(sample_count * full_length))
    return (point_grad, gradient.reshape(sequence_in.shape))


def solution(mesh):
    return jax.shard_map(
        shards,
        mesh=mesh,
        in_specs=(
            P("dp", "seq", None),
            P("dp", "seq", None),
            P("dp", None),
            P(),
            P(),
            P(),
            P(),
            P(None, None, "seq", None),
            P("seq", None, None),
        ),
        out_specs=(P("seq", None, None), P("dp", "seq", None)),
        check_vma=False,
    )
```

```python
import functools
import math

import jax
import jax.numpy as jnp
from jax import lax
from jax.experimental import pallas as pl
from jax.experimental.pallas import tpu as pltpu
from jax.sharding import PartitionSpec as P

FIRST_DILATION = 1024
SECOND_DILATION = 2048


def passed_along(value, axis, by):
    peers = lax.axis_size(axis)
    pairs = [(i, i + by) for i in range(peers) if 0 <= i + by < peers]
    return lax.ppermute(value, axis, pairs)


def gelu_tanh(values):
    return jax.nn.gelu(values, approximate=True)


def contract_last(left, right):
    return lax.dot_general(
        left, right, (((1,), (1,)), ((), ())), preferred_element_type=jnp.float32
    )


def neighbours(source, shards_away):
    if shards_away >= lax.axis_size("seq"):
        return (jnp.zeros_like(source), jnp.zeros_like(source))
    earlier = passed_along(source, "seq", shards_away)
    later = passed_along(source, "seq", -shards_away)
    return (earlier, later)


def forward_local(
    state, earlier, activated, later, weight, gain_vec, offset_vec, projection, kept_flag
):
    conv_out = jnp.dot(earlier, weight[0], preferred_element_type=jnp.float32)
    conv_out = conv_out + jnp.dot(activated, weight[1], preferred_element_type=jnp.float32)
    conv_out = conv_out + jnp.dot(later, weight[2], preferred_element_type=jnp.float32)
    middle = conv_out * gain_vec + offset_vec
    hidden_act = gelu_tanh(middle).astype(jnp.bfloat16)
    branch = jnp.dot(hidden_act, projection, preferred_element_type=jnp.float32)
    result = (state.astype(jnp.float32) + kept_flag * branch).astype(jnp.bfloat16)
    return (middle, hidden_act, result)


def backward_first(gradient, middle, projection, gain_vec, kept_flag):
    branch_grad = (kept_flag * gradient.astype(jnp.float32)).astype(jnp.bfloat16)
    hidden_grad = contract_last(branch_grad, projection)
    middle_grad = jax.vjp(gelu_tanh, middle)[1](hidden_grad)[0]
    conv_grad = (middle_grad * gain_vec).astype(jnp.bfloat16)
    return (conv_grad, branch_grad)


def backward_second(gradient, earlier, conv_grad, later, weight, normed, gain_vec):
    act_grad = (
        contract_last(later, weight[0])
        + contract_last(conv_grad, weight[1])
        + contract_last(earlier, weight[2])
    )
    normed_grad = jax.vjp(gelu_tanh, normed)[1](act_grad)[0] * gain_vec
    return (gradient.astype(jnp.float32) + normed_grad).astype(jnp.bfloat16)


def grad_rows(hidden_act, branch_grad):
    return lax.dot_general(
        hidden_act, branch_grad, (((0,), (0,)), ((), ())), preferred_element_type=jnp.float32
    )


MESH = pl.DeviceIdType.MESH
CHUNKS = 2
PIECES = 5
TANH_SCALE = 0.7978845608028654
CUBIC = 0.044715


def gelu_and_slope(values):
    squared = values * values
    tanh = jnp.tanh(values * (TANH_SCALE + (TANH_SCALE * CUBIC) * squared))
    gate = 0.5 + 0.5 * tanh
    bend = values * (0.5 - 0.5 * tanh * tanh)
    slope = gate + bend * (TANH_SCALE + (3.0 * TANH_SCALE * CUBIC) * squared)
    return values * gate, slope


def gelu_only(values):
    tanh = jnp.tanh(values * (TANH_SCALE + (TANH_SCALE * CUBIC) * (values * values)))
    return values * (0.5 + 0.5 * tanh)


def dot(left, right):
    return jnp.dot(left, right, preferred_element_type=jnp.float32)


def paired_kernel(
    scale,
    x_hbm,
    og_hbm,
    skip_ref,
    in_gain_ref,
    in_shift_ref,
    mid_gain_ref,
    mid_offset_ref,
    cw_ref,
    pw_ref,
    pg_ref,
    gin_ref,
    x_ref,
    og_ref,
    points,
    wbuf,
    wpoint,
    act0,
    slope0,
    own_conv,
    hidden_grad1,
    part_out,
    part_in,
    cgrad_out,
    cgrad_in,
    hidden0,
    hidden1,
    bgrad0,
    bgrad1,
    grad1,
    term,
    term_out,
    core_in,
    y_out,
    y_in,
    x_out,
    x_in,
    z_keep,
    z_out,
    z_in,
    final,
    ssem,
    rsem,
    lsem,
):
    seq = lax.axis_index("seq")
    dp = lax.axis_index("dp")
    core = seq % 2
    xpos = seq // 2
    ypos = dp % 2
    zpos = dp // 2
    depth = z_in.shape[0]
    core_mate = {"seq": seq + 1 - 2 * core}
    x_mate = {"seq": (seq + 2) % 4}
    y_mate = {"dp": dp + 1 - 2 * ypos}
    z_mates = [{"dp": (dp + 2 * j) % (2 * depth)} for j in range(1, depth)]
    rows = x_ref.shape[0]
    size = rows // CHUNKS
    channels = x_ref.shape[1]
    hidden = own_conv.shape[1]
    tap = 2 * xpos

    barrier = pltpu.get_barrier_semaphore()
    peers = [core_mate, x_mate, y_mate] + z_mates
    for peer in peers:
        pl.semaphore_signal(barrier, inc=1, device_id=peer, device_id_type=MESH)

    def local(src, dst, index):
        return pltpu.make_async_copy(src, dst, lsem.at[index])

    load_x = local(x_hbm, x_ref, 0)
    load_og = local(og_hbm, og_ref, 1)
    load_x.start()
    load_og.start()
    for b in range(2):
        points[b] = pw_ref[:, b, :].reshape(points.shape[1:])
    pl.semaphore_wait(barrier, len(peers))

    def remote(src, dst, index, peer):
        return pltpu.make_async_remote_copy(
            src_ref=src,
            dst_ref=dst,
            send_sem=ssem.at[index],
            recv_sem=rsem.at[index],
            device_id=peer,
            device_id_type=MESH,
        )

    def mine(piece, for_mate):
        if piece == 0:
            return cw_ref.at[0, 2 - tap if for_mate else tap]
        return (None, cw_ref.at[0, 1], points.at[0], cw_ref.at[1, 1], points.at[1])[piece]

    def place(piece, owner):
        where = (wbuf.at[0], wbuf.at[1], wpoint.at[0], wbuf.at[2], wpoint.at[1])[piece]
        return where.at[owner]

    far = (seq + 2) % 4
    to_core, to_x, to_y, fwd_x, fwd_y = [], [], [], [], []
    for k in range(PIECES):
        to_core.append(remote(mine(k, False), place(k, seq), 5 * k, core_mate))
        if k == 0:
            to_x.append(remote(mine(k, True), place(k, seq), 1, x_mate))
            fwd_x.append(remote(place(k, far), place(k, far), 3, core_mate))
            continue
        to_x.append(
            remote(mine(k, True).at[ypos], place(k, seq).at[ypos], 5 * k + 1, x_mate)
        )
        half = place(k, far).at[ypos]
        to_y.append(remote(half, half, 5 * k + 2, y_mate))
        fwd_x.append(remote(half, half, 5 * k + 3, core_mate))
        other = place(k, far).at[1 - ypos]
        fwd_y.append(remote(other, other, 5 * k + 4, core_mate))
    own = [local(mine(k, False), place(k, seq), 2 + k) for k in range(PIECES)]
    for k in range(PIECES):
        to_x[k].start()
        to_core[k].start()
        own[k].start()

    def after_x(k):
        to_x[k].wait_recv()
        fwd_x[k].start()
        if k > 0:
            to_y[k - 1].start()

    def after_y(k):
        to_y[k - 1].wait_recv()
        fwd_y[k - 1].start()

    def ready(k):
        own[k].wait()
        to_core[k].wait_recv()
        fwd_x[k].wait_recv()
        if k > 0:
            fwd_y[k - 1].wait_recv()

    keep = [(1 - skip_ref[0, b]).astype(jnp.float32) for b in range(2)]
    in_gain = [in_gain_ref[b : b + 1, :] for b in range(2)]
    in_shift = [in_shift_ref[b : b + 1, :] for b in range(2)]
    mid_gain = [mid_gain_ref[b : b + 1, :] for b in range(2)]
    mid_offset = [mid_offset_ref[b : b + 1, :] for b in range(2)]

    def conv_full(k):
        return wbuf[k].reshape(channels, hidden)

    def point_full(b):
        return wpoint[b].reshape(hidden, channels)

    def at(r):
        return pl.ds(pl.multiple_of(r * size, size), size)

    def chunked(body):
        def step(r, carry):
            body(r)
            return carry

        lax.fori_loop(0, CHUNKS, step, 0)

    def start_block(r):
        spot = at(r)
        value = x_ref[spot, :].astype(jnp.float32) * in_gain[0] + in_shift[0]
        gelu, slope = gelu_and_slope(value)
        act0[spot, :] = gelu.astype(jnp.bfloat16)
        slope0[spot, :] = slope * in_gain[0]
        bgrad1[spot, :] = (keep[1] * og_ref[spot, :].astype(jnp.float32)).astype(jnp.bfloat16)

    load_x.wait()
    load_og.wait()
    chunked(start_block)

    part_base = 5 * PIECES
    cgrad_base = part_base + CHUNKS
    term_base = cgrad_base + CHUNKS

    def part_copy(r):
        return remote(part_out.at[at(r)], part_in.at[at(r)], part_base + r, x_mate)

    def cgrad_copy(r):
        return remote(cgrad_out.at[at(r)], cgrad_in.at[at(r)], cgrad_base + r, x_mate)

    after_x(0)
    after_x(1)
    ready(0)

    def make_part(r):
        spot = at(r)
        part_out[spot, :] = dot(act0[spot, :], conv_full(0)).astype(jnp.bfloat16)
        part_copy(r).start()

    chunked(make_part)
    after_y(1)
    after_x(2)
    after_x(3)
    after_y(2)
    ready(1)

    def make_own(r):
        spot = at(r)
        own_conv[spot, :] = dot(act0[spot, :], conv_full(1))

    chunked(make_own)
    after_x(4)
    after_y(3)
    after_y(4)
    ready(4)

    def make_hidden_grad(r):
        spot = at(r)
        hidden_grad1[spot, :] = contract_last(bgrad1[spot, :], point_full(1))

    chunked(make_hidden_grad)
    ready(2)
    ready(3)

    def middle_part(r):
        spot = at(r)
        part_copy(r).wait_recv()
        conv = own_conv[spot, :] + part_in[spot, :].astype(jnp.float32)
        gelu, mid_slope0 = gelu_and_slope(conv * mid_gain[0] + mid_offset[0])
        act_hidden0 = gelu.astype(jnp.bfloat16)
        hidden0[spot, :] = act_hidden0
        branch = dot(act_hidden0, point_full(0))
        state = (x_ref[spot, :].astype(jnp.float32) + keep[0] * branch).astype(jnp.bfloat16)
        gelu, slope1 = gelu_and_slope(state.astype(jnp.float32) * in_gain[1] + in_shift[1])
        conv = dot(gelu.astype(jnp.bfloat16), conv_full(2))
        gelu, mid_slope1 = gelu_and_slope(conv * mid_gain[1] + mid_offset[1])
        hidden1[spot, :] = gelu.astype(jnp.bfloat16)
        conv_grad = (mid_slope1 * hidden_grad1[spot, :] * mid_gain[1]).astype(jnp.bfloat16)
        act_grad = contract_last(conv_grad, conv_full(2))
        gradient = (
            og_ref[spot, :].astype(jnp.float32) + slope1 * act_grad * in_gain[1]
        ).astype(jnp.bfloat16)
        grad1[spot, :] = gradient
        branch_grad = (keep[0] * gradient.astype(jnp.float32)).astype(jnp.bfloat16)
        bgrad0[spot, :] = branch_grad
        hidden_grad = contract_last(branch_grad, point_full(0))
        cgrad_out[spot, :] = (mid_slope0 * hidden_grad * mid_gain[0]).astype(jnp.bfloat16)
        cgrad_copy(r).start()

    share = hidden // 4
    half_cols = channels // 2

    def add_terms(r, b):
        spot = slice(r * size, (r + 1) * size)
        kept, branch = ((hidden0, bgrad0), (hidden1, bgrad1))[b]
        product = grad_rows(kept[spot, :], branch[spot, :])
        for owner in range(4):
            for col in range(2):
                block = product[
                    owner * share : (owner + 1) * share, col * half_cols : (col + 1) * half_cols
                ]
                where = (b, owner % 2, col, owner // 2)
                if r > 0:
                    block = block + term[where]
                term[where] = block
                if r == CHUNKS - 1:
                    term_out[where] = block.astype(jnp.bfloat16)

    core_copy = [
        remote(term_out.at[b, 1 - core], core_in.at[b], term_base + b, core_mate)
        for b in range(2)
    ]
    y_copy = [remote(y_out.at[b], y_in.at[b], term_base + 2 + b, y_mate) for b in range(2)]
    x_copy = [remote(x_out.at[b], x_in.at[b], term_base + 4 + b, x_mate) for b in range(2)]
    z_base = term_base + 6
    z_copy = [
        remote(z_out.at[(zpos + j) % depth], z_in.at[j], z_base + j - 1, z_mates[j - 1])
        for j in range(1, depth)
    ]
    gather_base = z_base + depth - 1
    own_quarter = final.at[ypos, zpos]
    z_gather = [
        remote(own_quarter, own_quarter, gather_base + j - 1, z_mates[j - 1])
        for j in range(1, depth)
    ]
    y_gather = []
    for j in range(depth):
        quarter = final.at[ypos, (zpos + depth - j) % depth]
        y_gather.append(remote(quarter, quarter, gather_base + depth - 1 + j, y_mate))

    def last_part(r):
        spot = at(r)
        cgrad_copy(r).wait_recv()
        act_grad = contract_last(cgrad_out[spot, :], conv_full(1))
        act_grad = act_grad + contract_last(cgrad_in[spot, :], conv_full(0))
        gin_ref[spot, :] = (
            grad1[spot, :].astype(jnp.float32) + slope0[spot, :] * act_grad
        ).astype(jnp.bfloat16)

    for r in range(CHUNKS):
        middle_part(r)
        for b in (1, 0):
            add_terms(r, b)
            if r == CHUNKS - 1:
                core_copy[b].start()

    for b in (1, 0):
        core_copy[b].wait_recv()
        away = term[b, core, 1 - ypos] + core_in[b, 1 - ypos].astype(jnp.float32)
        y_out[b] = away.astype(jnp.bfloat16)
        y_copy[b].start()
    last_part(0)
    for b in (1, 0):
        y_copy[b].wait_recv()
        away = term[b, core, ypos, 1 - xpos] + core_in[b, ypos, 1 - xpos].astype(jnp.float32)
        x_out[b] = (away + y_in[b, 1 - xpos].astype(jnp.float32)).astype(jnp.bfloat16)
        x_copy[b].start()
    last_part(1)
    half_rows = share // 2
    for b in (1, 0):
        near = term[b, core, ypos, xpos] + core_in[b, ypos, xpos].astype(jnp.float32)
        near = near + y_in[b, xpos].astype(jnp.float32)
        x_copy[b].wait_recv()
        near = near + x_in[b].astype(jnp.float32)
        for part in range(2):
            block = near[part * half_rows : (part + 1) * half_rows, :]
            z_keep[2 * b + part] = block
            z_out[2 * b + part] = block.astype(jnp.bfloat16)
    for copy in z_copy:
        copy.start()
    total = z_keep[zpos]
    for j in range(1, depth):
        z_copy[j - 1].wait_recv()
        total = total + z_in[j].astype(jnp.float32)
    final[ypos, zpos] = total.astype(jnp.bfloat16)
    for copy in z_gather:
        copy.start()
    y_gather[0].start()
    for j in range(1, depth):
        z_gather[j - 1].wait_recv()
        y_gather[j].start()
    for copy in y_gather:
        copy.wait_recv()
    for b in range(2):
        for part in range(2):
            for col in range(2):
                block = final[col, 2 * b + part].astype(jnp.float32) * scale
                spot = slice(part * half_rows, (part + 1) * half_rows)
                pg_ref[spot, b, col * half_cols : (col + 1) * half_cols] = block

    sums = (core_copy, x_copy, y_copy, z_copy, z_gather, y_gather)
    for group in (to_core, to_x, to_y, fwd_x, fwd_y) + sums:
        for copy in group:
            copy.wait_send()
    for r in range(CHUNKS):
        part_copy(r).wait_send()
        cgrad_copy(r).wait_send()


def paired_shards(
    sequence_in,
    output_grad,
    skip_mask,
    in_gain,
    input_shift_vec,
    mid_gain,
    mid_offset,
    conv_weight,
    point_weight,
):
    rows, channels = sequence_in.shape[1:]
    hidden = conv_weight.shape[3]
    share = point_weight.shape[0]
    depth = lax.axis_size("dp") // 2
    taps = conv_weight.reshape(2, 3, 2, -1, hidden)
    taps_shape = taps.shape[2:]
    points_shape = (2, share // 2, channels)
    copies = 5 * PIECES + 2 * CHUNKS + 6 + 3 * depth
    vmem = pl.BlockSpec(memory_space=pltpu.VMEM)
    hbm = pl.BlockSpec(memory_space=pltpu.HBM)
    smem = pl.BlockSpec(memory_space=pltpu.SMEM)
    bf16, f32 = jnp.bfloat16, jnp.float32
    quarter = (share // 2, channels // 2)
    half = (share, channels // 2)
    scratch = [
        pltpu.VMEM((rows, channels), bf16),
        pltpu.VMEM((rows, channels), bf16),
        pltpu.VMEM((2,) + points_shape, bf16),
        pltpu.VMEM((3, 4) + taps_shape, bf16),
        pltpu.VMEM((2, 4) + points_shape, bf16),
        pltpu.VMEM((rows, channels), bf16),
        pltpu.VMEM((rows, channels), f32),
        pltpu.VMEM((rows, hidden), f32),
        pltpu.VMEM((rows, hidden), f32),
        pltpu.VMEM((rows, hidden), bf16),
        pltpu.VMEM((rows, hidden), bf16),
        pltpu.VMEM((rows, hidden), bf16),
        pltpu.VMEM((rows, hidden), bf16),
        pltpu.VMEM((rows, hidden), bf16),
        pltpu.VMEM((rows, hidden), bf16),
        pltpu.VMEM((rows, channels), bf16),
        pltpu.VMEM((rows, channels), bf16),
        pltpu.VMEM((rows, channels), bf16),
        pltpu.VMEM((2, 2, 2, 2) + half, f32),
        pltpu.VMEM((2, 2, 2, 2) + half, bf16),
        pltpu.VMEM((2, 2, 2) + half, bf16),
        pltpu.VMEM((2, 2) + half, bf16),
        pltpu.VMEM((2, 2) + half, bf16),
        pltpu.VMEM((2,) + half, bf16),
        pltpu.VMEM((2,) + half, bf16),
        pltpu.VMEM((depth,) + quarter, f32),
        pltpu.VMEM((depth,) + quarter, bf16),
        pltpu.VMEM((depth,) + quarter, bf16),
        pltpu.VMEM((2, depth) + quarter, bf16),
        pltpu.SemaphoreType.DMA((copies,)),
        pltpu.SemaphoreType.DMA((copies,)),
        pltpu.SemaphoreType.DMA((2 + PIECES,)),
    ]
    sample_count = sequence_in.shape[0] * lax.axis_size("dp")
    full_length = rows * lax.axis_size("seq")
    scale = 1.0 / math.sqrt(sample_count * full_length)
    point_grad, gradient = pl.pallas_call(
        functools.partial(paired_kernel, scale),
        out_shape=(
            jax.ShapeDtypeStruct((share, 2, channels), f32),
            jax.ShapeDtypeStruct((rows, channels), bf16),
        ),
        in_specs=[hbm, hbm, smem] + [vmem] * 4 + [hbm, vmem],
        out_specs=(vmem, vmem),
        scratch_shapes=scratch,
        compiler_params=pltpu.CompilerParams(
            collective_id=0, has_side_effects=True, vmem_limit_bytes=48 * 2**20
        ),
    )(
        sequence_in.reshape(rows, channels),
        output_grad.reshape(rows, channels),
        skip_mask,
        in_gain,
        input_shift_vec,
        mid_gain,
        mid_offset,
        taps,
        point_weight,
    )
    return (point_grad, gradient.reshape(sequence_in.shape))


def pairs_apply(sequence_in):
    count, positions = sequence_in.shape[:2]
    peers = lax.axis_size("seq")
    reach = (FIRST_DILATION // positions, SECOND_DILATION // positions)
    return (
        count == 1
        and peers == 4
        and lax.axis_size("dp") == 8
        and 2 * reach[0] == peers
        and reach[1] >= peers
    )


def shards(
    sequence_in,
    output_grad,
    skip_mask,
    in_gain,
    input_shift_vec,
    mid_gain,
    mid_offset,
    conv_weight,
    point_weight,
):
    if pairs_apply(sequence_in):
        return paired_shards(
            sequence_in,
            output_grad,
            skip_mask,
            in_gain,
            input_shift_vec,
            mid_gain,
            mid_offset,
            conv_weight,
            point_weight,
        )
    position_list = sequence_in.shape[1]
    channels = sequence_in.shape[2]
    point_full = lax.all_gather(point_weight, "seq", axis=0, tiled=True)
    neighbour_reach = (FIRST_DILATION // position_list, SECOND_DILATION // position_list)
    state = sequence_in.reshape(-1, channels)
    total_rows = state.shape[0]
    saved = []
    kept_weights = []
    for block_index in range(2):
        kept_flag = (1 - skip_mask[0, block_index]).astype(jnp.float32)
        normed = state.astype(jnp.float32) * in_gain[block_index] + input_shift_vec[block_index]
        activated = gelu_tanh(normed).astype(jnp.bfloat16)
        earlier, later = neighbours(
            activated.reshape(sequence_in.shape), neighbour_reach[block_index]
        )
        earlier = earlier.reshape(total_rows, channels)
        later = later.reshape(total_rows, channels)
        weight = lax.all_gather(conv_weight[block_index], "seq", axis=1, tiled=True)
        kept_weights.append(weight)
        operands = (
            state,
            earlier,
            activated,
            later,
            weight,
            mid_gain[block_index],
            mid_offset[block_index],
            point_full[:, block_index, :],
            kept_flag,
        )
        middle, hidden_act, state = forward_local(*operands)
        saved.append((normed, middle, hidden_act, kept_flag))
    gradient = output_grad.reshape(-1, channels)
    hidden_saved = [None, None]
    branch_saved = [None, None]
    for block_index in (1, 0):
        normed, middle, hidden_act, kept_flag = saved[block_index]
        projection = point_full[:, block_index, :]
        first_operands = (gradient, middle, projection, mid_gain[block_index], kept_flag)
        conv_grad, branch_grad = backward_first(*first_operands)
        hidden_saved[block_index] = hidden_act
        branch_saved[block_index] = branch_grad
        earlier, later = neighbours(
            conv_grad.reshape(sequence_in.shape[0], position_list, -1), neighbour_reach[block_index]
        )
        earlier = earlier.reshape(total_rows, -1)
        later = later.reshape(total_rows, -1)
        weight = lax.all_gather(conv_weight[block_index], "seq", axis=1, tiled=True)
        second_operands = (
            gradient,
            earlier,
            conv_grad,
            later,
            weight,
            normed,
            in_gain[block_index],
        )
        gradient = backward_second(*second_operands)
    first_term = grad_rows(hidden_saved[0], branch_saved[0])
    second_term = grad_rows(hidden_saved[1], branch_saved[1])
    shared_part = lax.psum_scatter(
        jnp.stack([first_term, second_term], axis=1), "seq", scatter_dimension=0, tiled=True
    )
    summed = lax.psum(shared_part, "dp")
    sample_count = sequence_in.shape[0] * lax.axis_size("dp")
    full_length = position_list * lax.axis_size("seq")
    point_grad = summed * (1.0 / math.sqrt(sample_count * full_length))
    return (point_grad, gradient.reshape(sequence_in.shape))


def solution(mesh):
    return jax.shard_map(
        shards,
        mesh=mesh,
        in_specs=(
            P("dp", "seq", None),
            P("dp", "seq", None),
            P("dp", None),
            P(),
            P(),
            P(),
            P(),
            P(None, None, "seq", None),
            P("seq", None, None),
        ),
        out_specs=(P("seq", None, None), P("dp", "seq", None)),
        check_vma=False,
    )
```

```python
import functools
import math

import jax
import jax.numpy as jnp
from jax import lax
from jax.experimental import pallas as pl
from jax.experimental.pallas import tpu as pltpu
from jax.sharding import PartitionSpec as P

FIRST_DILATION = 1024
SECOND_DILATION = 2048


def passed_along(value, axis, by):
    peers = lax.axis_size(axis)
    pairs = [(i, i + by) for i in range(peers) if 0 <= i + by < peers]
    return lax.ppermute(value, axis, pairs)


def gelu_tanh(values):
    return jax.nn.gelu(values, approximate=True)


def contract_last(left, right):
    return lax.dot_general(
        left, right, (((1,), (1,)), ((), ())), preferred_element_type=jnp.float32
    )


def neighbours(source, shards_away):
    if shards_away >= lax.axis_size("seq"):
        return (jnp.zeros_like(source), jnp.zeros_like(source))
    earlier = passed_along(source, "seq", shards_away)
    later = passed_along(source, "seq", -shards_away)
    return (earlier, later)


def forward_local(
    state, earlier, activated, later, weight, gain_vec, offset_vec, projection, kept_flag
):
    conv_out = jnp.dot(earlier, weight[0], preferred_element_type=jnp.float32)
    conv_out = conv_out + jnp.dot(activated, weight[1], preferred_element_type=jnp.float32)
    conv_out = conv_out + jnp.dot(later, weight[2], preferred_element_type=jnp.float32)
    middle = conv_out * gain_vec + offset_vec
    hidden_act = gelu_tanh(middle).astype(jnp.bfloat16)
    branch = jnp.dot(hidden_act, projection, preferred_element_type=jnp.float32)
    result = (state.astype(jnp.float32) + kept_flag * branch).astype(jnp.bfloat16)
    return (middle, hidden_act, result)


def backward_first(gradient, middle, projection, gain_vec, kept_flag):
    branch_grad = (kept_flag * gradient.astype(jnp.float32)).astype(jnp.bfloat16)
    hidden_grad = contract_last(branch_grad, projection)
    middle_grad = jax.vjp(gelu_tanh, middle)[1](hidden_grad)[0]
    conv_grad = (middle_grad * gain_vec).astype(jnp.bfloat16)
    return (conv_grad, branch_grad)


def backward_second(gradient, earlier, conv_grad, later, weight, normed, gain_vec):
    act_grad = (
        contract_last(later, weight[0])
        + contract_last(conv_grad, weight[1])
        + contract_last(earlier, weight[2])
    )
    normed_grad = jax.vjp(gelu_tanh, normed)[1](act_grad)[0] * gain_vec
    return (gradient.astype(jnp.float32) + normed_grad).astype(jnp.bfloat16)


def grad_rows(hidden_act, branch_grad):
    return lax.dot_general(
        hidden_act, branch_grad, (((0,), (0,)), ((), ())), preferred_element_type=jnp.float32
    )


MESH = pl.DeviceIdType.MESH
CHUNKS = 2
PIECES = 5
TANH_SCALE = 0.7978845608028654
CUBIC = 0.044715


def gelu_and_slope(values):
    squared = values * values
    tanh = jnp.tanh(values * (TANH_SCALE + (TANH_SCALE * CUBIC) * squared))
    gate = 0.5 + 0.5 * tanh
    bend = values * (0.5 - 0.5 * tanh * tanh)
    slope = gate + bend * (TANH_SCALE + (3.0 * TANH_SCALE * CUBIC) * squared)
    return values * gate, slope


def gelu_only(values):
    tanh = jnp.tanh(values * (TANH_SCALE + (TANH_SCALE * CUBIC) * (values * values)))
    return values * (0.5 + 0.5 * tanh)


def dot(left, right):
    return jnp.dot(left, right, preferred_element_type=jnp.float32)


def paired_kernel(
    scale,
    x_hbm,
    og_hbm,
    skip_ref,
    in_gain_hbm,
    in_shift_hbm,
    mid_gain_hbm,
    mid_offset_hbm,
    cw_ref,
    pw_hbm,
    pg_hbm,
    gin_hbm,
    in_gain_ref,
    in_shift_ref,
    mid_gain_ref,
    mid_offset_ref,
    pw_ref,
    pg_ref,
    gin_ref,
    x_ref,
    og_ref,
    points,
    wbuf,
    wpoint,
    act0,
    slope0,
    own_conv,
    hidden_grad1,
    part_out,
    part_in,
    cgrad_out,
    cgrad_in,
    hidden0,
    hidden1,
    bgrad0,
    bgrad1,
    grad1,
    term,
    term_out,
    core_in,
    one_out,
    one_in,
    two_out,
    two_in,
    z_keep,
    z_out,
    z_in,
    final,
    ssem,
    rsem,
    lsem,
):
    seq = lax.axis_index("seq")
    dp = lax.axis_index("dp")
    core = seq % 2
    xpos = seq // 2
    ypos = dp % 2
    zpos = dp // 2
    depth = z_in.shape[0]
    core_mate = {"seq": seq + 1 - 2 * core}
    x_mate = {"seq": (seq + 2) % 4}
    y_mate = {"dp": dp + 1 - 2 * ypos}
    z_mates = [{"dp": (dp + 2 * j) % (2 * depth)} for j in range(1, depth)]
    rows = x_ref.shape[0]
    size = rows // CHUNKS
    channels = x_ref.shape[1]
    hidden = own_conv.shape[1]
    tap = 2 * xpos

    barrier = pltpu.get_barrier_semaphore()
    peers = [core_mate, x_mate, y_mate] + z_mates
    for peer in peers:
        pl.semaphore_signal(barrier, inc=1, device_id=peer, device_id_type=MESH)

    def local(src, dst, index):
        return pltpu.make_async_copy(src, dst, lsem.at[index])

    load_points = local(pw_hbm, pw_ref, 0)
    loads = [
        local(x_hbm, x_ref, 1),
        local(og_hbm, og_ref, 2),
        local(in_gain_hbm, in_gain_ref, 3),
        local(in_shift_hbm, in_shift_ref, 4),
        local(mid_gain_hbm, mid_gain_ref, 5),
        local(mid_offset_hbm, mid_offset_ref, 6),
    ]
    load_points.start()
    for load in loads:
        load.start()
    pl.semaphore_wait(barrier, len(peers))

    def remote(src, dst, index, peer):
        return pltpu.make_async_remote_copy(
            src_ref=src,
            dst_ref=dst,
            send_sem=ssem.at[index],
            recv_sem=rsem.at[index],
            device_id=peer,
            device_id_type=MESH,
        )

    def mine(piece, for_mate):
        if piece == 0:
            return cw_ref.at[0, 2 - tap if for_mate else tap]
        return (None, cw_ref.at[0, 1], points.at[0], cw_ref.at[1, 1], points.at[1])[piece]

    def place(piece, owner):
        where = (wbuf.at[0], wbuf.at[1], wpoint.at[0], wbuf.at[2], wpoint.at[1])[piece]
        return where.at[owner]

    far = (seq + 2) % 4
    zlow = zpos % 2
    z_near = {"dp": dp + 2 - 4 * zlow}

    def quarter_of(half, which):
        if half.shape[1] == hidden:
            count = half.shape[0] // 2
            return half.at[pl.ds(pl.multiple_of(which * count, count), count)]
        count = half.shape[1] // 2
        return half.at[:, pl.ds(pl.multiple_of(which * count, count), count)]

    to_core, to_x, to_z, to_y, fwd_x, fwd_y = [], [], [], [], [], []
    for k in range(PIECES):
        to_core.append(remote(mine(k, False), place(k, seq), 6 * k, core_mate))
        if k == 0:
            to_x.append(remote(mine(k, True), place(k, seq), 1, x_mate))
            fwd_x.append(remote(place(k, far), place(k, far), 3, core_mate))
            continue
        near_quarter = quarter_of(mine(k, True).at[ypos], zlow)
        to_x.append(
            remote(near_quarter, quarter_of(place(k, seq).at[ypos], zlow), 6 * k + 1, x_mate)
        )
        half = place(k, far).at[ypos]
        quarter = quarter_of(half, zlow)
        to_z.append(remote(quarter, quarter, 6 * k + 5, z_near))
        to_y.append(remote(half, half, 6 * k + 2, y_mate))
        fwd_x.append(remote(half, half, 6 * k + 3, core_mate))
        other = place(k, far).at[1 - ypos]
        fwd_y.append(remote(other, other, 6 * k + 4, core_mate))
    own = [local(mine(k, False), place(k, seq), 7 + k) for k in range(PIECES)]
    for k in range(PIECES):
        if k == 2:
            load_points.wait()
            for b in range(2):
                points[b] = pw_ref[:, b, :].reshape(points.shape[1:])
        to_x[k].start()
        to_core[k].start()
        own[k].start()

    def after_x(k):
        to_x[k].wait_recv()
        if k == 0:
            fwd_x[0].start()
        else:
            to_z[k - 1].start()

    def after_z(k):
        to_z[k - 1].wait_recv()
        to_y[k - 1].start()
        fwd_x[k].start()

    def after_y(k):
        to_y[k - 1].wait_recv()
        fwd_y[k - 1].start()

    def ready(k):
        own[k].wait()
        to_core[k].wait_recv()
        fwd_x[k].wait_recv()
        if k > 0:
            fwd_y[k - 1].wait_recv()

    for load in loads:
        load.wait()
    keep = [(1 - skip_ref[0, b]).astype(jnp.float32) for b in range(2)]
    in_gain = [in_gain_ref[b : b + 1, :] for b in range(2)]
    in_shift = [in_shift_ref[b : b + 1, :] for b in range(2)]
    mid_gain = [mid_gain_ref[b : b + 1, :] for b in range(2)]
    mid_offset = [mid_offset_ref[b : b + 1, :] for b in range(2)]

    def conv_full(k):
        return wbuf[k].reshape(channels, hidden)

    def point_full(b):
        return wpoint[b].reshape(hidden, channels)

    def at(r):
        return pl.ds(pl.multiple_of(r * size, size), size)

    def chunked(body):
        def step(r, carry):
            body(r)
            return carry

        lax.fori_loop(0, CHUNKS, step, 0)

    def start_block(r):
        spot = at(r)
        value = x_ref[spot, :].astype(jnp.float32) * in_gain[0] + in_shift[0]
        gelu, slope = gelu_and_slope(value)
        act0[spot, :] = gelu.astype(jnp.bfloat16)
        slope0[spot, :] = slope * in_gain[0]
        bgrad1[spot, :] = (keep[1] * og_ref[spot, :].astype(jnp.float32)).astype(jnp.bfloat16)

    chunked(start_block)

    part_base = 6 * PIECES
    cgrad_base = part_base + CHUNKS
    term_base = cgrad_base + CHUNKS

    def part_copy(r):
        return remote(part_out.at[at(r)], part_in.at[at(r)], part_base + r, x_mate)

    def cgrad_copy(r):
        return remote(cgrad_out.at[at(r)], cgrad_in.at[at(r)], cgrad_base + r, x_mate)

    after_x(0)
    after_x(1)
    after_x(2)
    ready(0)

    def make_part(r):
        spot = at(r)
        part_out[spot, :] = dot(act0[spot, :], conv_full(0)).astype(jnp.bfloat16)
        part_copy(r).start()

    chunked(make_part)
    after_x(3)
    after_x(4)
    for k in range(1, PIECES):
        after_z(k)
    after_y(1)
    ready(1)

    def make_own(r):
        spot = at(r)
        own_conv[spot, :] = dot(act0[spot, :], conv_full(1))

    chunked(make_own)
    for k in range(2, PIECES):
        after_y(k)
    ready(4)

    def make_hidden_grad(r):
        spot = at(r)
        hidden_grad1[spot, :] = contract_last(bgrad1[spot, :], point_full(1))

    chunked(make_hidden_grad)
    ready(2)
    ready(3)

    def middle_part(r):
        spot = at(r)
        part_copy(r).wait_recv()
        conv = own_conv[spot, :] + part_in[spot, :].astype(jnp.float32)
        gelu, mid_slope0 = gelu_and_slope(conv * mid_gain[0] + mid_offset[0])
        act_hidden0 = gelu.astype(jnp.bfloat16)
        hidden0[spot, :] = act_hidden0
        branch = dot(act_hidden0, point_full(0))
        state = (x_ref[spot, :].astype(jnp.float32) + keep[0] * branch).astype(jnp.bfloat16)
        gelu, slope1 = gelu_and_slope(state.astype(jnp.float32) * in_gain[1] + in_shift[1])
        conv = dot(gelu.astype(jnp.bfloat16), conv_full(2))
        gelu, mid_slope1 = gelu_and_slope(conv * mid_gain[1] + mid_offset[1])
        hidden1[spot, :] = gelu.astype(jnp.bfloat16)
        conv_grad = (mid_slope1 * hidden_grad1[spot, :] * mid_gain[1]).astype(jnp.bfloat16)
        act_grad = contract_last(conv_grad, conv_full(2))
        gradient = (
            og_ref[spot, :].astype(jnp.float32) + slope1 * act_grad * in_gain[1]
        ).astype(jnp.bfloat16)
        grad1[spot, :] = gradient
        branch_grad = (keep[0] * gradient.astype(jnp.float32)).astype(jnp.bfloat16)
        bgrad0[spot, :] = branch_grad
        hidden_grad = contract_last(branch_grad, point_full(0))
        cgrad_out[spot, :] = (mid_slope0 * hidden_grad * mid_gain[0]).astype(jnp.bfloat16)
        if r < CHUNKS - 1:
            cgrad_copy(r).start()

    share = hidden // 4
    half_cols = channels // 2

    def add_terms(r, b):
        spot = slice(r * size, (r + 1) * size)
        kept, branch = ((hidden0, bgrad0), (hidden1, bgrad1))[b]
        product = grad_rows(kept[spot, :], branch[spot, :])
        for owner in range(4):
            for col in range(2):
                block = product[
                    owner * share : (owner + 1) * share, col * half_cols : (col + 1) * half_cols
                ]
                first, second = (col, owner // 2) if b == 1 else (owner // 2, col)
                where = (b, owner % 2, first, second)
                if r > 0:
                    block = block + term[where]
                term[where] = block
                if r == CHUNKS - 1:
                    term_out[where] = block.astype(jnp.bfloat16)

    core_copy = [
        remote(term_out.at[b, 1 - core], core_in.at[b], term_base + b, core_mate)
        for b in range(2)
    ]
    ways = ((xpos, ypos, x_mate, y_mate), (ypos, xpos, y_mate, x_mate))
    one_copy = [remote(one_out.at[b], one_in.at[b], term_base + 2 + b, ways[b][2]) for b in range(2)]
    two_copy = [remote(two_out.at[b], two_in.at[b], term_base + 4 + b, ways[b][3]) for b in range(2)]
    z_base = term_base + 6
    z_copy = [
        remote(z_out.at[(zpos + j) % depth], z_in.at[j], z_base + j - 1, z_mates[j - 1])
        for j in range(1, depth)
    ]
    gather_base = z_base + depth - 1
    own_quarter = final.at[ypos, zpos]
    z_gather = [
        remote(own_quarter, own_quarter, gather_base + j - 1, z_mates[j - 1])
        for j in range(1, depth)
    ]
    y_gather = []
    for j in range(depth):
        quarter = final.at[ypos, (zpos + depth - j) % depth]
        y_gather.append(remote(quarter, quarter, gather_base + depth - 1 + j, y_mate))

    def last_part(r):
        spot = at(r)
        cgrad_copy(r).wait_recv()
        act_grad = contract_last(cgrad_out[spot, :], conv_full(1))
        act_grad = act_grad + contract_last(cgrad_in[spot, :], conv_full(0))
        gin_ref[spot, :] = (
            grad1[spot, :].astype(jnp.float32) + slope0[spot, :] * act_grad
        ).astype(jnp.bfloat16)
        gin_copy(r).start()

    def gin_copy(r):
        return local(gin_ref.at[at(r)], gin_hbm.at[at(r)], 7 + PIECES + r)

    for r in range(CHUNKS):
        middle_part(r)
        for b in (1, 0):
            add_terms(r, b)
            if r == CHUNKS - 1:
                core_copy[b].start()

    for b in (1, 0):
        first = ways[b][0]
        core_copy[b].wait_recv()
        away = term[b, core, 1 - first] + core_in[b, 1 - first].astype(jnp.float32)
        one_out[b] = away.astype(jnp.bfloat16)
        one_copy[b].start()
    last_part(0)
    for b in (1, 0):
        first, second = ways[b][:2]
        one_copy[b].wait_recv()
        away = term[b, core, first, 1 - second]
        away = away + core_in[b, first, 1 - second].astype(jnp.float32)
        away = away + one_in[b, 1 - second].astype(jnp.float32)
        two_out[b] = away.astype(jnp.bfloat16)
        two_copy[b].start()
    cgrad_copy(CHUNKS - 1).start()
    half_rows = share // 2
    for b in (1, 0):
        first, second = ways[b][:2]
        near = term[b, core, first, second] + core_in[b, first, second].astype(jnp.float32)
        near = near + one_in[b, second].astype(jnp.float32)
        two_copy[b].wait_recv()
        near = near + two_in[b].astype(jnp.float32)
        for part in range(2):
            block = near[part * half_rows : (part + 1) * half_rows, :]
            z_keep[2 * b + part] = block
            z_out[2 * b + part] = block.astype(jnp.bfloat16)
    for copy in z_copy:
        copy.start()
    last_part(1)
    total = z_keep[zpos]
    for j in range(1, depth):
        z_copy[j - 1].wait_recv()
        total = total + z_in[j].astype(jnp.float32)
    final[ypos, zpos] = total.astype(jnp.bfloat16)
    for copy in z_gather:
        copy.start()
    y_gather[0].start()
    for j in range(1, depth):
        z_gather[j - 1].wait_recv()
        y_gather[j].start()
    for copy in y_gather:
        copy.wait_recv()
    for b in range(2):
        for part in range(2):
            for col in range(2):
                block = final[col, 2 * b + part].astype(jnp.float32) * scale
                spot = slice(part * half_rows, (part + 1) * half_rows)
                pg_ref[spot, b, col * half_cols : (col + 1) * half_cols] = block

    pg_copy = local(pg_ref, pg_hbm, 7 + PIECES + CHUNKS)
    pg_copy.start()
    sums = (core_copy, one_copy, two_copy, z_copy, z_gather, y_gather)
    for group in (to_core, to_x, to_z, to_y, fwd_x, fwd_y) + sums:
        for copy in group:
            copy.wait_send()
    for r in range(CHUNKS):
        part_copy(r).wait_send()
        cgrad_copy(r).wait_send()
        gin_copy(r).wait()
    pg_copy.wait()


def paired_shards(
    sequence_in,
    output_grad,
    skip_mask,
    in_gain,
    input_shift_vec,
    mid_gain,
    mid_offset,
    conv_weight,
    point_weight,
):
    rows, channels = sequence_in.shape[1:]
    hidden = conv_weight.shape[3]
    share = point_weight.shape[0]
    depth = lax.axis_size("dp") // 2
    taps = conv_weight.reshape(2, 3, 2, -1, hidden)
    taps_shape = taps.shape[2:]
    points_shape = (2, share // 2, channels)
    copies = 6 * PIECES + 2 * CHUNKS + 6 + 3 * depth
    hbm = pl.BlockSpec(memory_space=pltpu.HBM)
    smem = pl.BlockSpec(memory_space=pltpu.SMEM)
    bf16, f32 = jnp.bfloat16, jnp.float32
    quarter = (share // 2, channels // 2)
    half = (share, channels // 2)
    scratch = [
        pltpu.VMEM(in_gain.shape, f32),
        pltpu.VMEM(in_gain.shape, f32),
        pltpu.VMEM(mid_gain.shape, f32),
        pltpu.VMEM(mid_gain.shape, f32),
        pltpu.VMEM(point_weight.shape, bf16),
        pltpu.VMEM((share, 2, channels), f32),
        pltpu.VMEM((rows, channels), bf16),
        pltpu.VMEM((rows, channels), bf16),
        pltpu.VMEM((rows, channels), bf16),
        pltpu.VMEM((2,) + points_shape, bf16),
        pltpu.VMEM((3, 4) + taps_shape, bf16),
        pltpu.VMEM((2, 4) + points_shape, bf16),
        pltpu.VMEM((rows, channels), bf16),
        pltpu.VMEM((rows, channels), f32),
        pltpu.VMEM((rows, hidden), f32),
        pltpu.VMEM((rows, hidden), f32),
        pltpu.VMEM((rows, hidden), bf16),
        pltpu.VMEM((rows, hidden), bf16),
        pltpu.VMEM((rows, hidden), bf16),
        pltpu.VMEM((rows, hidden), bf16),
        pltpu.VMEM((rows, hidden), bf16),
        pltpu.VMEM((rows, hidden), bf16),
        pltpu.VMEM((rows, channels), bf16),
        pltpu.VMEM((rows, channels), bf16),
        pltpu.VMEM((rows, channels), bf16),
        pltpu.VMEM((2, 2, 2, 2) + half, f32),
        pltpu.VMEM((2, 2, 2, 2) + half, bf16),
        pltpu.VMEM((2, 2, 2) + half, bf16),
        pltpu.VMEM((2, 2) + half, bf16),
        pltpu.VMEM((2, 2) + half, bf16),
        pltpu.VMEM((2,) + half, bf16),
        pltpu.VMEM((2,) + half, bf16),
        pltpu.VMEM((depth,) + quarter, f32),
        pltpu.VMEM((depth,) + quarter, bf16),
        pltpu.VMEM((depth,) + quarter, bf16),
        pltpu.VMEM((2, depth) + quarter, bf16),
        pltpu.SemaphoreType.DMA((copies,)),
        pltpu.SemaphoreType.DMA((copies,)),
        pltpu.SemaphoreType.DMA((8 + PIECES + CHUNKS,)),
    ]
    sample_count = sequence_in.shape[0] * lax.axis_size("dp")
    full_length = rows * lax.axis_size("seq")
    scale = 1.0 / math.sqrt(sample_count * full_length)
    point_grad, gradient = pl.pallas_call(
        functools.partial(paired_kernel, scale),
        out_shape=(
            jax.ShapeDtypeStruct((share, 2, channels), f32),
            jax.ShapeDtypeStruct((rows, channels), bf16),
        ),
        in_specs=[hbm, hbm, smem] + [hbm] * 6,
        out_specs=(hbm, hbm),
        scratch_shapes=scratch,
        compiler_params=pltpu.CompilerParams(
            collective_id=0, has_side_effects=True, vmem_limit_bytes=62 * 2**20
        ),
    )(
        sequence_in.reshape(rows, channels),
        output_grad.reshape(rows, channels),
        skip_mask,
        in_gain,
        input_shift_vec,
        mid_gain,
        mid_offset,
        taps,
        point_weight,
    )
    return (point_grad, gradient.reshape(sequence_in.shape))


def pairs_apply(sequence_in):
    count, positions = sequence_in.shape[:2]
    peers = lax.axis_size("seq")
    reach = (FIRST_DILATION // positions, SECOND_DILATION // positions)
    return (
        count == 1
        and peers == 4
        and lax.axis_size("dp") == 8
        and 2 * reach[0] == peers
        and reach[1] >= peers
    )


def shards(
    sequence_in,
    output_grad,
    skip_mask,
    in_gain,
    input_shift_vec,
    mid_gain,
    mid_offset,
    conv_weight,
    point_weight,
):
    if pairs_apply(sequence_in):
        return paired_shards(
            sequence_in,
            output_grad,
            skip_mask,
            in_gain,
            input_shift_vec,
            mid_gain,
            mid_offset,
            conv_weight,
            point_weight,
        )
    position_list = sequence_in.shape[1]
    channels = sequence_in.shape[2]
    point_full = lax.all_gather(point_weight, "seq", axis=0, tiled=True)
    neighbour_reach = (FIRST_DILATION // position_list, SECOND_DILATION // position_list)
    state = sequence_in.reshape(-1, channels)
    total_rows = state.shape[0]
    saved = []
    kept_weights = []
    for block_index in range(2):
        kept_flag = (1 - skip_mask[0, block_index]).astype(jnp.float32)
        normed = state.astype(jnp.float32) * in_gain[block_index] + input_shift_vec[block_index]
        activated = gelu_tanh(normed).astype(jnp.bfloat16)
        earlier, later = neighbours(
            activated.reshape(sequence_in.shape), neighbour_reach[block_index]
        )
        earlier = earlier.reshape(total_rows, channels)
        later = later.reshape(total_rows, channels)
        weight = lax.all_gather(conv_weight[block_index], "seq", axis=1, tiled=True)
        kept_weights.append(weight)
        operands = (
            state,
            earlier,
            activated,
            later,
            weight,
            mid_gain[block_index],
            mid_offset[block_index],
            point_full[:, block_index, :],
            kept_flag,
        )
        middle, hidden_act, state = forward_local(*operands)
        saved.append((normed, middle, hidden_act, kept_flag))
    gradient = output_grad.reshape(-1, channels)
    hidden_saved = [None, None]
    branch_saved = [None, None]
    for block_index in (1, 0):
        normed, middle, hidden_act, kept_flag = saved[block_index]
        projection = point_full[:, block_index, :]
        first_operands = (gradient, middle, projection, mid_gain[block_index], kept_flag)
        conv_grad, branch_grad = backward_first(*first_operands)
        hidden_saved[block_index] = hidden_act
        branch_saved[block_index] = branch_grad
        earlier, later = neighbours(
            conv_grad.reshape(sequence_in.shape[0], position_list, -1), neighbour_reach[block_index]
        )
        earlier = earlier.reshape(total_rows, -1)
        later = later.reshape(total_rows, -1)
        weight = lax.all_gather(conv_weight[block_index], "seq", axis=1, tiled=True)
        second_operands = (
            gradient,
            earlier,
            conv_grad,
            later,
            weight,
            normed,
            in_gain[block_index],
        )
        gradient = backward_second(*second_operands)
    first_term = grad_rows(hidden_saved[0], branch_saved[0])
    second_term = grad_rows(hidden_saved[1], branch_saved[1])
    shared_part = lax.psum_scatter(
        jnp.stack([first_term, second_term], axis=1), "seq", scatter_dimension=0, tiled=True
    )
    summed = lax.psum(shared_part, "dp")
    sample_count = sequence_in.shape[0] * lax.axis_size("dp")
    full_length = position_list * lax.axis_size("seq")
    point_grad = summed * (1.0 / math.sqrt(sample_count * full_length))
    return (point_grad, gradient.reshape(sequence_in.shape))


def solution(mesh):
    return jax.shard_map(
        shards,
        mesh=mesh,
        in_specs=(
            P("dp", "seq", None),
            P("dp", "seq", None),
            P("dp", None),
            P(),
            P(),
            P(),
            P(),
            P(None, None, "seq", None),
            P("seq", None, None),
        ),
        out_specs=(P("seq", None, None), P("dp", "seq", None)),
        check_vma=False,
    )
```

```python
import functools
import math

import jax
import jax.numpy as jnp
from jax import lax
from jax.experimental import pallas as pl
from jax.experimental.pallas import tpu as pltpu
from jax.sharding import PartitionSpec as P

FIRST_DILATION = 1024
SECOND_DILATION = 2048


def passed_along(value, axis, by):
    peers = lax.axis_size(axis)
    pairs = [(i, i + by) for i in range(peers) if 0 <= i + by < peers]
    return lax.ppermute(value, axis, pairs)


def gelu_tanh(values):
    return jax.nn.gelu(values, approximate=True)


def contract_last(left, right):
    return lax.dot_general(
        left, right, (((1,), (1,)), ((), ())), preferred_element_type=jnp.float32
    )


def neighbours(source, shards_away):
    if shards_away >= lax.axis_size("seq"):
        return (jnp.zeros_like(source), jnp.zeros_like(source))
    earlier = passed_along(source, "seq", shards_away)
    later = passed_along(source, "seq", -shards_away)
    return (earlier, later)


def forward_local(
    state, earlier, activated, later, weight, gain_vec, offset_vec, projection, kept_flag
):
    conv_out = jnp.dot(earlier, weight[0], preferred_element_type=jnp.float32)
    conv_out = conv_out + jnp.dot(activated, weight[1], preferred_element_type=jnp.float32)
    conv_out = conv_out + jnp.dot(later, weight[2], preferred_element_type=jnp.float32)
    middle = conv_out * gain_vec + offset_vec
    hidden_act = gelu_tanh(middle).astype(jnp.bfloat16)
    branch = jnp.dot(hidden_act, projection, preferred_element_type=jnp.float32)
    result = (state.astype(jnp.float32) + kept_flag * branch).astype(jnp.bfloat16)
    return (middle, hidden_act, result)


def backward_first(gradient, middle, projection, gain_vec, kept_flag):
    branch_grad = (kept_flag * gradient.astype(jnp.float32)).astype(jnp.bfloat16)
    hidden_grad = contract_last(branch_grad, projection)
    middle_grad = jax.vjp(gelu_tanh, middle)[1](hidden_grad)[0]
    conv_grad = (middle_grad * gain_vec).astype(jnp.bfloat16)
    return (conv_grad, branch_grad)


def backward_second(gradient, earlier, conv_grad, later, weight, normed, gain_vec):
    act_grad = (
        contract_last(later, weight[0])
        + contract_last(conv_grad, weight[1])
        + contract_last(earlier, weight[2])
    )
    normed_grad = jax.vjp(gelu_tanh, normed)[1](act_grad)[0] * gain_vec
    return (gradient.astype(jnp.float32) + normed_grad).astype(jnp.bfloat16)


def grad_rows(hidden_act, branch_grad):
    return lax.dot_general(
        hidden_act, branch_grad, (((0,), (0,)), ((), ())), preferred_element_type=jnp.float32
    )


MESH = pl.DeviceIdType.MESH
CHUNKS = 2
PIECES = 5
TANH_SCALE = 0.7978845608028654
CUBIC = 0.044715


def gelu_and_slope(values):
    squared = values * values
    tanh = jnp.tanh(values * (TANH_SCALE + (TANH_SCALE * CUBIC) * squared))
    gate = 0.5 + 0.5 * tanh
    bend = values * (0.5 - 0.5 * tanh * tanh)
    slope = gate + bend * (TANH_SCALE + (3.0 * TANH_SCALE * CUBIC) * squared)
    return values * gate, slope


def gelu_only(values):
    tanh = jnp.tanh(values * (TANH_SCALE + (TANH_SCALE * CUBIC) * (values * values)))
    return values * (0.5 + 0.5 * tanh)


def dot(left, right):
    return jnp.dot(left, right, preferred_element_type=jnp.float32)


def paired_kernel(
    scale,
    x_hbm,
    og_hbm,
    skip_ref,
    in_gain_hbm,
    in_shift_hbm,
    mid_gain_hbm,
    mid_offset_hbm,
    cw_ref,
    pw_hbm,
    pg_hbm,
    gin_hbm,
    in_gain_ref,
    in_shift_ref,
    mid_gain_ref,
    mid_offset_ref,
    pw_ref,
    pg_ref,
    gin_ref,
    x_ref,
    og_ref,
    points,
    wbuf,
    wpoint,
    act0,
    slope0,
    own_conv,
    part_out,
    part_in,
    cgrad_out,
    cgrad_in,
    hidden0,
    hidden1,
    bgrad0,
    bgrad1,
    grad1,
    term,
    term_out,
    core_in,
    one_out,
    one_in,
    two_out,
    two_in,
    z_keep,
    z_out,
    z_in,
    final,
    ssem,
    rsem,
    lsem,
):
    seq = lax.axis_index("seq")
    dp = lax.axis_index("dp")
    core = seq % 2
    xpos = seq // 2
    ypos = dp % 2
    zpos = dp // 2
    depth = z_in.shape[0]
    core_mate = {"seq": seq + 1 - 2 * core}
    x_mate = {"seq": (seq + 2) % 4}
    y_mate = {"dp": dp + 1 - 2 * ypos}
    z_mates = [{"dp": (dp + 2 * j) % (2 * depth)} for j in range(1, depth)]
    rows = x_ref.shape[0]
    size = rows // CHUNKS
    channels = x_ref.shape[1]
    hidden = own_conv.shape[1]
    tap = 2 * xpos

    barrier = pltpu.get_barrier_semaphore()
    peers = [core_mate, x_mate, y_mate] + z_mates
    for peer in peers:
        pl.semaphore_signal(barrier, inc=1, device_id=peer, device_id_type=MESH)

    def local(src, dst, index):
        return pltpu.make_async_copy(src, dst, lsem.at[index])

    load_points = local(pw_hbm, pw_ref, 0)
    loads = [
        local(x_hbm, x_ref, 1),
        local(og_hbm, og_ref, 2),
        local(in_gain_hbm, in_gain_ref, 3),
        local(in_shift_hbm, in_shift_ref, 4),
        local(mid_gain_hbm, mid_gain_ref, 5),
        local(mid_offset_hbm, mid_offset_ref, 6),
    ]
    load_points.start()
    for load in loads:
        load.start()
    pl.semaphore_wait(barrier, len(peers))

    def remote(src, dst, index, peer):
        return pltpu.make_async_remote_copy(
            src_ref=src,
            dst_ref=dst,
            send_sem=ssem.at[index],
            recv_sem=rsem.at[index],
            device_id=peer,
            device_id_type=MESH,
        )

    def mine(piece, for_mate):
        if piece == 0:
            return cw_ref.at[0, 2 - tap if for_mate else tap]
        return (None, cw_ref.at[0, 1], points.at[0], cw_ref.at[1, 1], points.at[1])[piece]

    def place(piece, owner):
        where = (wbuf.at[0], wbuf.at[1], wpoint.at[0], wbuf.at[2], wpoint.at[1])[piece]
        return where.at[owner]

    far = (seq + 2) % 4
    zlow = zpos % 2
    z_near = {"dp": dp + 2 - 4 * zlow}

    def quarter_of(half, which):
        if half.shape[1] == hidden:
            count = half.shape[0] // 2
            return half.at[pl.ds(pl.multiple_of(which * count, count), count)]
        count = half.shape[1] // 2
        return half.at[:, pl.ds(pl.multiple_of(which * count, count), count)]

    to_core, to_x, to_z, to_y, fwd_x, fwd_y = [], [], [], [], [], []
    for k in range(PIECES):
        to_core.append(remote(mine(k, False), place(k, seq), 6 * k, core_mate))
        if k == 0:
            to_x.append(remote(mine(k, True), place(k, seq), 1, x_mate))
            fwd_x.append(remote(place(k, far), place(k, far), 3, core_mate))
            continue
        near_quarter = quarter_of(mine(k, True).at[ypos], zlow)
        to_x.append(
            remote(near_quarter, quarter_of(place(k, seq).at[ypos], zlow), 6 * k + 1, x_mate)
        )
        half = place(k, far).at[ypos]
        quarter = quarter_of(half, zlow)
        to_z.append(remote(quarter, quarter, 6 * k + 5, z_near))
        to_y.append(remote(half, half, 6 * k + 2, y_mate))
        fwd_x.append(remote(half, half, 6 * k + 3, core_mate))
        other = place(k, far).at[1 - ypos]
        fwd_y.append(remote(other, other, 6 * k + 4, core_mate))
    own = [local(mine(k, False), place(k, seq), 7 + k) for k in range(PIECES)]

    def send_piece(k):
        to_x[k].start()
        to_core[k].start()
        own[k].start()

    send_piece(0)
    load_points.wait()
    for b in range(2):
        points[b] = pw_ref[:, b, :].reshape(points.shape[1:])

    def after_x(k):
        to_x[k].wait_recv()
        if k == 0:
            fwd_x[0].start()
        else:
            to_z[k - 1].start()

    def after_z(k):
        to_z[k - 1].wait_recv()
        to_y[k - 1].start()
        fwd_x[k].start()

    def after_y(k):
        to_y[k - 1].wait_recv()
        fwd_y[k - 1].start()

    def ready(k):
        own[k].wait()
        to_core[k].wait_recv()
        fwd_x[k].wait_recv()
        if k > 0:
            fwd_y[k - 1].wait_recv()

    for load in loads:
        load.wait()
    keep = [(1 - skip_ref[0, b]).astype(jnp.float32) for b in range(2)]
    in_gain = [in_gain_ref[b : b + 1, :] for b in range(2)]
    in_shift = [in_shift_ref[b : b + 1, :] for b in range(2)]
    mid_gain = [mid_gain_ref[b : b + 1, :] for b in range(2)]
    mid_offset = [mid_offset_ref[b : b + 1, :] for b in range(2)]

    def conv_full(k):
        return wbuf[k].reshape(channels, hidden)

    def point_full(b):
        return wpoint[b].reshape(hidden, channels)

    def at(r):
        return pl.ds(pl.multiple_of(r * size, size), size)

    def chunked(body):
        def step(r, carry):
            body(r)
            return carry

        lax.fori_loop(0, CHUNKS, step, 0)

    def start_block(r):
        spot = at(r)
        value = x_ref[spot, :].astype(jnp.float32) * in_gain[0] + in_shift[0]
        gelu, slope = gelu_and_slope(value)
        act0[spot, :] = gelu.astype(jnp.bfloat16)
        slope0[spot, :] = slope * in_gain[0]
        bgrad1[spot, :] = (keep[1] * og_ref[spot, :].astype(jnp.float32)).astype(jnp.bfloat16)

    for r in range(CHUNKS):
        send_piece(1 + r)
        start_block(r)
    for k in range(1 + CHUNKS, PIECES):
        send_piece(k)

    part_base = 6 * PIECES
    cgrad_base = part_base + CHUNKS
    term_base = cgrad_base + CHUNKS

    def part_copy(r):
        return remote(part_out.at[at(r)], part_in.at[at(r)], part_base + r, x_mate)

    def cgrad_copy(r):
        return remote(cgrad_out.at[at(r)], cgrad_in.at[at(r)], cgrad_base + r, x_mate)

    after_x(0)
    after_x(1)
    after_x(2)
    ready(0)

    def make_part(r):
        spot = at(r)
        part_out[spot, :] = dot(act0[spot, :], conv_full(0)).astype(jnp.bfloat16)
        part_copy(r).start()

    chunked(make_part)
    after_z(1)
    after_x(3)
    after_z(2)
    after_x(4)
    after_y(1)
    after_z(3)
    after_z(4)
    ready(1)

    def make_own(r):
        spot = at(r)
        own_conv[spot, :] = dot(act0[spot, :], conv_full(1))

    chunked(make_own)
    after_y(2)
    ready(2)

    def middle_part(r):
        spot = at(r)
        part_copy(r).wait_recv()
        conv = own_conv[spot, :] + part_in[spot, :].astype(jnp.float32)
        gelu, mid_slope0 = gelu_and_slope(conv * mid_gain[0] + mid_offset[0])
        act_hidden0 = gelu.astype(jnp.bfloat16)
        hidden0[spot, :] = act_hidden0
        branch = dot(act_hidden0, point_full(0))
        state = (x_ref[spot, :].astype(jnp.float32) + keep[0] * branch).astype(jnp.bfloat16)
        gelu, slope1 = gelu_and_slope(state.astype(jnp.float32) * in_gain[1] + in_shift[1])
        if r == 0:
            after_y(3)
            ready(3)
        conv = dot(gelu.astype(jnp.bfloat16), conv_full(2))
        gelu, mid_slope1 = gelu_and_slope(conv * mid_gain[1] + mid_offset[1])
        hidden1[spot, :] = gelu.astype(jnp.bfloat16)
        if r == 0:
            after_y(4)
            ready(4)
        hidden_grad = contract_last(bgrad1[spot, :], point_full(1))
        conv_grad = (mid_slope1 * hidden_grad * mid_gain[1]).astype(jnp.bfloat16)
        act_grad = contract_last(conv_grad, conv_full(2))
        gradient = (
            og_ref[spot, :].astype(jnp.float32) + slope1 * act_grad * in_gain[1]
        ).astype(jnp.bfloat16)
        grad1[spot, :] = gradient
        branch_grad = (keep[0] * gradient.astype(jnp.float32)).astype(jnp.bfloat16)
        bgrad0[spot, :] = branch_grad
        hidden_grad = contract_last(branch_grad, point_full(0))
        cgrad_out[spot, :] = (mid_slope0 * hidden_grad * mid_gain[0]).astype(jnp.bfloat16)
        if r < CHUNKS - 1:
            cgrad_copy(r).start()

    share = hidden // 4
    half_cols = channels // 2

    def add_terms(r, b):
        spot = slice(r * size, (r + 1) * size)
        kept, branch = ((hidden0, bgrad0), (hidden1, bgrad1))[b]
        product = grad_rows(kept[spot, :], branch[spot, :])
        for owner in range(4):
            for col in range(2):
                block = product[
                    owner * share : (owner + 1) * share, col * half_cols : (col + 1) * half_cols
                ]
                first, second = (col, owner // 2) if b == 1 else (owner // 2, col)
                where = (b, owner % 2, first, second)
                if r > 0:
                    block = block + term[where]
                term[where] = block
                if r == CHUNKS - 1:
                    term_out[where] = block.astype(jnp.bfloat16)

    core_copy = [
        remote(term_out.at[b, 1 - core], core_in.at[b], term_base + b, core_mate)
        for b in range(2)
    ]
    ways = ((xpos, ypos, x_mate, y_mate), (ypos, xpos, y_mate, x_mate))
    one_copy = [remote(one_out.at[b], one_in.at[b], term_base + 2 + b, ways[b][2]) for b in range(2)]
    two_copy = [remote(two_out.at[b], two_in.at[b], term_base + 4 + b, ways[b][3]) for b in range(2)]
    z_base = term_base + 6
    z_copy = [
        remote(z_out.at[(zpos + j) % depth], z_in.at[j], z_base + j - 1, z_mates[j - 1])
        for j in range(1, depth)
    ]
    gather_base = z_base + depth - 1
    own_quarter = final.at[ypos, zpos]
    z_gather = [
        remote(own_quarter, own_quarter, gather_base + j - 1, z_mates[j - 1])
        for j in range(1, depth)
    ]
    y_gather = []
    for j in range(depth):
        quarter = final.at[ypos, (zpos + depth - j) % depth]
        y_gather.append(remote(quarter, quarter, gather_base + depth - 1 + j, y_mate))

    def last_part(r):
        spot = at(r)
        cgrad_copy(r).wait_recv()
        act_grad = contract_last(cgrad_out[spot, :], conv_full(1))
        act_grad = act_grad + contract_last(cgrad_in[spot, :], conv_full(0))
        gin_ref[spot, :] = (
            grad1[spot, :].astype(jnp.float32) + slope0[spot, :] * act_grad
        ).astype(jnp.bfloat16)
        gin_copy(r).start()

    def gin_copy(r):
        return local(gin_ref.at[at(r)], gin_hbm.at[at(r)], 7 + PIECES + r)

    for r in range(CHUNKS):
        middle_part(r)
        for b in (1, 0):
            add_terms(r, b)
            if r == CHUNKS - 1:
                core_copy[b].start()

    for b in (1, 0):
        first = ways[b][0]
        core_copy[b].wait_recv()
        away = term[b, core, 1 - first] + core_in[b, 1 - first].astype(jnp.float32)
        one_out[b] = away.astype(jnp.bfloat16)
        one_copy[b].start()
    last_part(0)
    for b in (1, 0):
        first, second = ways[b][:2]
        one_copy[b].wait_recv()
        away = term[b, core, first, 1 - second]
        away = away + core_in[b, first, 1 - second].astype(jnp.float32)
        away = away + one_in[b, 1 - second].astype(jnp.float32)
        two_out[b] = away.astype(jnp.bfloat16)
        two_copy[b].start()
    cgrad_copy(CHUNKS - 1).start()
    half_rows = share // 2
    for b in (1, 0):
        first, second = ways[b][:2]
        near = term[b, core, first, second] + core_in[b, first, second].astype(jnp.float32)
        near = near + one_in[b, second].astype(jnp.float32)
        two_copy[b].wait_recv()
        near = near + two_in[b].astype(jnp.float32)
        for part in range(2):
            block = near[part * half_rows : (part + 1) * half_rows, :]
            z_keep[2 * b + part] = block
            z_out[2 * b + part] = block.astype(jnp.bfloat16)
    for copy in z_copy:
        copy.start()
    last_part(1)
    total = z_keep[zpos]
    for j in range(1, depth):
        z_copy[j - 1].wait_recv()
        total = total + z_in[j].astype(jnp.float32)
    final[ypos, zpos] = total.astype(jnp.bfloat16)
    for copy in z_gather:
        copy.start()
    y_gather[0].start()

    def settle(col, which):
        block = final[col, which].astype(jnp.float32) * scale
        for q in range(depth):
            for side in range(2):

                @pl.when((which == q) & (col == side))
                def _():
                    spot = slice((q % 2) * half_rows, (q % 2 + 1) * half_rows)
                    pg_ref[spot, q // 2, side * half_cols : (side + 1) * half_cols] = block

    settle(ypos, zpos)
    for j in range(1, depth):
        z_gather[j - 1].wait_recv()
        y_gather[j].start()
    for j in range(1, depth):
        settle(ypos, (zpos + depth - j) % depth)
    for j in range(depth):
        y_gather[j].wait_recv()
        settle(1 - ypos, (zpos + depth - j) % depth)

    pg_copy = local(pg_ref, pg_hbm, 7 + PIECES + CHUNKS)
    pg_copy.start()
    sums = (core_copy, one_copy, two_copy, z_copy, z_gather, y_gather)
    for group in (to_core, to_x, to_z, to_y, fwd_x, fwd_y) + sums:
        for copy in group:
            copy.wait_send()
    for r in range(CHUNKS):
        part_copy(r).wait_send()
        cgrad_copy(r).wait_send()
        gin_copy(r).wait()
    pg_copy.wait()


def settle_kernel(pg_from, gin_from, pg_to, gin_to, sem):
    copies = []
    for index, (source, target) in enumerate(((pg_from, pg_to), (gin_from, gin_to))):
        count = source.shape[0] // 4
        for part in range(4):
            spot = pl.ds(part * count, count)
            copies.append(
                pltpu.make_async_copy(source.at[spot], target.at[spot], sem.at[4 * index + part])
            )
    for copy in copies:
        copy.start()
    for copy in copies:
        copy.wait()


def paired_shards(
    sequence_in,
    output_grad,
    skip_mask,
    in_gain,
    input_shift_vec,
    mid_gain,
    mid_offset,
    conv_weight,
    point_weight,
):
    rows, channels = sequence_in.shape[1:]
    hidden = conv_weight.shape[3]
    share = point_weight.shape[0]
    depth = lax.axis_size("dp") // 2
    taps = conv_weight.reshape(2, 3, 2, -1, hidden)
    taps_shape = taps.shape[2:]
    points_shape = (2, share // 2, channels)
    copies = 6 * PIECES + 2 * CHUNKS + 6 + 3 * depth
    hbm = pl.BlockSpec(memory_space=pltpu.HBM)
    smem = pl.BlockSpec(memory_space=pltpu.SMEM)
    bf16, f32 = jnp.bfloat16, jnp.float32
    quarter = (share // 2, channels // 2)
    half = (share, channels // 2)
    scratch = [
        pltpu.VMEM(in_gain.shape, f32),
        pltpu.VMEM(in_gain.shape, f32),
        pltpu.VMEM(mid_gain.shape, f32),
        pltpu.VMEM(mid_gain.shape, f32),
        pltpu.VMEM(point_weight.shape, bf16),
        pltpu.VMEM((share, 2, channels), f32),
        pltpu.VMEM((rows, channels), bf16),
        pltpu.VMEM((rows, channels), bf16),
        pltpu.VMEM((rows, channels), bf16),
        pltpu.VMEM((2,) + points_shape, bf16),
        pltpu.VMEM((3, 4) + taps_shape, bf16),
        pltpu.VMEM((2, 4) + points_shape, bf16),
        pltpu.VMEM((rows, channels), bf16),
        pltpu.VMEM((rows, channels), f32),
        pltpu.VMEM((rows, hidden), f32),
        pltpu.VMEM((rows, hidden), bf16),
        pltpu.VMEM((rows, hidden), bf16),
        pltpu.VMEM((rows, hidden), bf16),
        pltpu.VMEM((rows, hidden), bf16),
        pltpu.VMEM((rows, hidden), bf16),
        pltpu.VMEM((rows, hidden), bf16),
        pltpu.VMEM((rows, channels), bf16),
        pltpu.VMEM((rows, channels), bf16),
        pltpu.VMEM((rows, channels), bf16),
        pltpu.VMEM((2, 2, 2, 2) + half, f32),
        pltpu.VMEM((2, 2, 2, 2) + half, bf16),
        pltpu.VMEM((2, 2, 2) + half, bf16),
        pltpu.VMEM((2, 2) + half, bf16),
        pltpu.VMEM((2, 2) + half, bf16),
        pltpu.VMEM((2,) + half, bf16),
        pltpu.VMEM((2,) + half, bf16),
        pltpu.VMEM((depth,) + quarter, f32),
        pltpu.VMEM((depth,) + quarter, bf16),
        pltpu.VMEM((depth,) + quarter, bf16),
        pltpu.VMEM((2, depth) + quarter, bf16),
        pltpu.SemaphoreType.DMA((copies,)),
        pltpu.SemaphoreType.DMA((copies,)),
        pltpu.SemaphoreType.DMA((8 + PIECES + CHUNKS,)),
    ]
    sample_count = sequence_in.shape[0] * lax.axis_size("dp")
    full_length = rows * lax.axis_size("seq")
    scale = 1.0 / math.sqrt(sample_count * full_length)
    point_grad, gradient = pl.pallas_call(
        functools.partial(paired_kernel, scale),
        out_shape=(
            jax.ShapeDtypeStruct((share, 2, channels), f32),
            jax.ShapeDtypeStruct((rows, channels), bf16),
        ),
        in_specs=[hbm, hbm, smem] + [hbm] * 6,
        out_specs=(hbm, hbm),
        scratch_shapes=scratch,
        compiler_params=pltpu.CompilerParams(
            collective_id=0, has_side_effects=True, vmem_limit_bytes=62 * 2**20
        ),
    )(
        sequence_in.reshape(rows, channels),
        output_grad.reshape(rows, channels),
        skip_mask,
        in_gain,
        input_shift_vec,
        mid_gain,
        mid_offset,
        taps,
        point_weight,
    )
    point_grad, gradient = pl.pallas_call(
        settle_kernel,
        out_shape=(
            jax.ShapeDtypeStruct(point_grad.shape, f32),
            jax.ShapeDtypeStruct(gradient.shape, bf16),
        ),
        in_specs=[hbm, hbm],
        out_specs=(hbm, hbm),
        scratch_shapes=[pltpu.SemaphoreType.DMA((8,))],
        compiler_params=pltpu.CompilerParams(vmem_limit_bytes=62 * 2**20),
    )(point_grad, gradient)
    return (point_grad, gradient.reshape(sequence_in.shape))


def pairs_apply(sequence_in):
    count, positions = sequence_in.shape[:2]
    peers = lax.axis_size("seq")
    reach = (FIRST_DILATION // positions, SECOND_DILATION // positions)
    return (
        count == 1
        and peers == 4
        and lax.axis_size("dp") == 8
        and 2 * reach[0] == peers
        and reach[1] >= peers
    )


def shards(
    sequence_in,
    output_grad,
    skip_mask,
    in_gain,
    input_shift_vec,
    mid_gain,
    mid_offset,
    conv_weight,
    point_weight,
):
    if pairs_apply(sequence_in):
        return paired_shards(
            sequence_in,
            output_grad,
            skip_mask,
            in_gain,
            input_shift_vec,
            mid_gain,
            mid_offset,
            conv_weight,
            point_weight,
        )
    position_list = sequence_in.shape[1]
    channels = sequence_in.shape[2]
    point_full = lax.all_gather(point_weight, "seq", axis=0, tiled=True)
    neighbour_reach = (FIRST_DILATION // position_list, SECOND_DILATION // position_list)
    state = sequence_in.reshape(-1, channels)
    total_rows = state.shape[0]
    saved = []
    kept_weights = []
    for block_index in range(2):
        kept_flag = (1 - skip_mask[0, block_index]).astype(jnp.float32)
        normed = state.astype(jnp.float32) * in_gain[block_index] + input_shift_vec[block_index]
        activated = gelu_tanh(normed).astype(jnp.bfloat16)
        earlier, later = neighbours(
            activated.reshape(sequence_in.shape), neighbour_reach[block_index]
        )
        earlier = earlier.reshape(total_rows, channels)
        later = later.reshape(total_rows, channels)
        weight = lax.all_gather(conv_weight[block_index], "seq", axis=1, tiled=True)
        kept_weights.append(weight)
        operands = (
            state,
            earlier,
            activated,
            later,
            weight,
            mid_gain[block_index],
            mid_offset[block_index],
            point_full[:, block_index, :],
            kept_flag,
        )
        middle, hidden_act, state = forward_local(*operands)
        saved.append((normed, middle, hidden_act, kept_flag))
    gradient = output_grad.reshape(-1, channels)
    hidden_saved = [None, None]
    branch_saved = [None, None]
    for block_index in (1, 0):
        normed, middle, hidden_act, kept_flag = saved[block_index]
        projection = point_full[:, block_index, :]
        first_operands = (gradient, middle, projection, mid_gain[block_index], kept_flag)
        conv_grad, branch_grad = backward_first(*first_operands)
        hidden_saved[block_index] = hidden_act
        branch_saved[block_index] = branch_grad
        earlier, later = neighbours(
            conv_grad.reshape(sequence_in.shape[0], position_list, -1), neighbour_reach[block_index]
        )
        earlier = earlier.reshape(total_rows, -1)
        later = later.reshape(total_rows, -1)
        weight = lax.all_gather(conv_weight[block_index], "seq", axis=1, tiled=True)
        second_operands = (
            gradient,
            earlier,
            conv_grad,
            later,
            weight,
            normed,
            in_gain[block_index],
        )
        gradient = backward_second(*second_operands)
    first_term = grad_rows(hidden_saved[0], branch_saved[0])
    second_term = grad_rows(hidden_saved[1], branch_saved[1])
    shared_part = lax.psum_scatter(
        jnp.stack([first_term, second_term], axis=1), "seq", scatter_dimension=0, tiled=True
    )
    summed = lax.psum(shared_part, "dp")
    sample_count = sequence_in.shape[0] * lax.axis_size("dp")
    full_length = position_list * lax.axis_size("seq")
    point_grad = summed * (1.0 / math.sqrt(sample_count * full_length))
    return (point_grad, gradient.reshape(sequence_in.shape))


def solution(mesh):
    return jax.shard_map(
        shards,
        mesh=mesh,
        in_specs=(
            P("dp", "seq", None),
            P("dp", "seq", None),
            P("dp", None),
            P(),
            P(),
            P(),
            P(),
            P(None, None, "seq", None),
            P("seq", None, None),
        ),
        out_specs=(P("seq", None, None), P("dp", "seq", None)),
        check_vma=False,
    )
```

```python
import functools
import math

import jax
import jax.numpy as jnp
from jax import lax
from jax.experimental import pallas as pl
from jax.experimental.pallas import tpu as pltpu
from jax.sharding import PartitionSpec as P

FIRST_DILATION = 1024
SECOND_DILATION = 2048


def passed_along(value, axis, by):
    peers = lax.axis_size(axis)
    pairs = [(i, i + by) for i in range(peers) if 0 <= i + by < peers]
    return lax.ppermute(value, axis, pairs)


def gelu_tanh(values):
    return jax.nn.gelu(values, approximate=True)


def contract_last(left, right):
    return lax.dot_general(
        left, right, (((1,), (1,)), ((), ())), preferred_element_type=jnp.float32
    )


def neighbours(source, shards_away):
    if shards_away >= lax.axis_size("seq"):
        return (jnp.zeros_like(source), jnp.zeros_like(source))
    earlier = passed_along(source, "seq", shards_away)
    later = passed_along(source, "seq", -shards_away)
    return (earlier, later)


def forward_local(
    state, earlier, activated, later, weight, gain_vec, offset_vec, projection, kept_flag
):
    conv_out = jnp.dot(earlier, weight[0], preferred_element_type=jnp.float32)
    conv_out = conv_out + jnp.dot(activated, weight[1], preferred_element_type=jnp.float32)
    conv_out = conv_out + jnp.dot(later, weight[2], preferred_element_type=jnp.float32)
    middle = conv_out * gain_vec + offset_vec
    hidden_act = gelu_tanh(middle).astype(jnp.bfloat16)
    branch = jnp.dot(hidden_act, projection, preferred_element_type=jnp.float32)
    result = (state.astype(jnp.float32) + kept_flag * branch).astype(jnp.bfloat16)
    return (middle, hidden_act, result)


def backward_first(gradient, middle, projection, gain_vec, kept_flag):
    branch_grad = (kept_flag * gradient.astype(jnp.float32)).astype(jnp.bfloat16)
    hidden_grad = contract_last(branch_grad, projection)
    middle_grad = jax.vjp(gelu_tanh, middle)[1](hidden_grad)[0]
    conv_grad = (middle_grad * gain_vec).astype(jnp.bfloat16)
    return (conv_grad, branch_grad)


def backward_second(gradient, earlier, conv_grad, later, weight, normed, gain_vec):
    act_grad = (
        contract_last(later, weight[0])
        + contract_last(conv_grad, weight[1])
        + contract_last(earlier, weight[2])
    )
    normed_grad = jax.vjp(gelu_tanh, normed)[1](act_grad)[0] * gain_vec
    return (gradient.astype(jnp.float32) + normed_grad).astype(jnp.bfloat16)


def grad_rows(hidden_act, branch_grad):
    return lax.dot_general(
        hidden_act, branch_grad, (((0,), (0,)), ((), ())), preferred_element_type=jnp.float32
    )


MESH = pl.DeviceIdType.MESH
CHUNKS = 2
PIECES = 5
THROUGH_Z = (3, 4)
TANH_SCALE = 0.7978845608028654
CUBIC = 0.044715


def gelu_and_slope(values):
    squared = values * values
    tanh = jnp.tanh(values * (TANH_SCALE + (TANH_SCALE * CUBIC) * squared))
    gate = 0.5 + 0.5 * tanh
    bend = values * (0.5 - 0.5 * tanh * tanh)
    slope = gate + bend * (TANH_SCALE + (3.0 * TANH_SCALE * CUBIC) * squared)
    return values * gate, slope


def gelu_only(values):
    tanh = jnp.tanh(values * (TANH_SCALE + (TANH_SCALE * CUBIC) * (values * values)))
    return values * (0.5 + 0.5 * tanh)


def dot(left, right):
    return jnp.dot(left, right, preferred_element_type=jnp.float32)


def paired_kernel(
    scale,
    x_hbm,
    og_hbm,
    skip_ref,
    in_gain_hbm,
    in_shift_hbm,
    mid_gain_hbm,
    mid_offset_hbm,
    cw_ref,
    pw_hbm,
    pg_hbm,
    gin_hbm,
    in_gain_ref,
    in_shift_ref,
    mid_gain_ref,
    mid_offset_ref,
    pw_ref,
    pg_ref,
    gin_ref,
    x_ref,
    og_ref,
    points,
    wbuf,
    wpoint,
    act0,
    slope0,
    own_conv,
    part_out,
    part_in,
    cgrad_out,
    cgrad_in,
    hidden0,
    hidden1,
    bgrad0,
    bgrad1,
    grad1,
    term,
    term_out,
    core_in,
    one_out,
    one_in,
    two_out,
    two_in,
    z_keep,
    z_out,
    z_in,
    final,
    ssem,
    rsem,
    lsem,
):
    seq = lax.axis_index("seq")
    dp = lax.axis_index("dp")
    core = seq % 2
    xpos = seq // 2
    ypos = dp % 2
    zpos = dp // 2
    depth = z_in.shape[0]
    core_mate = {"seq": seq + 1 - 2 * core}
    x_mate = {"seq": (seq + 2) % 4}
    y_mate = {"dp": dp + 1 - 2 * ypos}
    z_mates = [{"dp": (dp + 2 * j) % (2 * depth)} for j in range(1, depth)]
    rows = x_ref.shape[0]
    size = rows // CHUNKS
    channels = x_ref.shape[1]
    hidden = own_conv.shape[1]
    tap = 2 * xpos

    barrier = pltpu.get_barrier_semaphore()
    peers = [core_mate, x_mate, y_mate] + z_mates
    for peer in peers:
        pl.semaphore_signal(barrier, inc=1, device_id=peer, device_id_type=MESH)

    def local(src, dst, index):
        return pltpu.make_async_copy(src, dst, lsem.at[index])

    load_points = local(pw_hbm, pw_ref, 0)
    loads = [
        local(x_hbm, x_ref, 1),
        local(og_hbm, og_ref, 2),
        local(in_gain_hbm, in_gain_ref, 3),
        local(in_shift_hbm, in_shift_ref, 4),
        local(mid_gain_hbm, mid_gain_ref, 5),
        local(mid_offset_hbm, mid_offset_ref, 6),
    ]
    load_points.start()
    for load in loads:
        load.start()
    pl.semaphore_wait(barrier, len(peers))

    def remote(src, dst, index, peer):
        return pltpu.make_async_remote_copy(
            src_ref=src,
            dst_ref=dst,
            send_sem=ssem.at[index],
            recv_sem=rsem.at[index],
            device_id=peer,
            device_id_type=MESH,
        )

    def mine(piece, for_mate):
        if piece == 0:
            return cw_ref.at[0, 2 - tap if for_mate else tap]
        return (None, cw_ref.at[0, 1], points.at[0], cw_ref.at[1, 1], points.at[1])[piece]

    def place(piece, owner):
        where = (wbuf.at[0], wbuf.at[1], wpoint.at[0], wbuf.at[2], wpoint.at[1])[piece]
        return where.at[owner]

    far = (seq + 2) % 4
    zlow = zpos % 2
    z_near = {"dp": dp + 2 - 4 * zlow}

    def quarter_of(half, which):
        if half.shape[1] == hidden:
            count = half.shape[0] // 2
            return half.at[pl.ds(pl.multiple_of(which * count, count), count)]
        count = half.shape[1] // 2
        return half.at[:, pl.ds(pl.multiple_of(which * count, count), count)]

    to_core, to_x, to_y, fwd_x, fwd_y = [], [], [], [], []
    to_z = {}
    for k in range(PIECES):
        to_core.append(remote(mine(k, False), place(k, seq), 6 * k, core_mate))
        if k == 0:
            to_x.append(remote(mine(k, True), place(k, seq), 1, x_mate))
            fwd_x.append(remote(place(k, far), place(k, far), 3, core_mate))
            continue
        half = place(k, far).at[ypos]
        mine_half, there = mine(k, True).at[ypos], place(k, seq).at[ypos]
        if k in THROUGH_Z:
            mine_half, there = quarter_of(mine_half, zlow), quarter_of(there, zlow)
            quarter = quarter_of(half, zlow)
            to_z[k] = remote(quarter, quarter, 6 * k + 5, z_near)
        to_x.append(remote(mine_half, there, 6 * k + 1, x_mate))
        to_y.append(remote(half, half, 6 * k + 2, y_mate))
        fwd_x.append(remote(half, half, 6 * k + 3, core_mate))
        other = place(k, far).at[1 - ypos]
        fwd_y.append(remote(other, other, 6 * k + 4, core_mate))
    own = [local(mine(k, False), place(k, seq), 7 + k) for k in range(PIECES)]

    def send_piece(k):
        to_x[k].start()
        to_core[k].start()
        own[k].start()

    send_piece(0)
    send_piece(1)
    load_points.wait()
    for b in range(2):
        points[b] = pw_ref[:, b, :].reshape(points.shape[1:])
    for k in range(2, PIECES):
        send_piece(k)

    def after_x(k):
        to_x[k].wait_recv()
        if k in THROUGH_Z:
            to_z[k].start()
            return
        fwd_x[k].start()
        if k > 0:
            to_y[k - 1].start()

    def after_z(k):
        to_z[k].wait_recv()
        to_y[k - 1].start()
        fwd_x[k].start()

    def after_y(k):
        to_y[k - 1].wait_recv()
        fwd_y[k - 1].start()

    def ready(k):
        own[k].wait()
        to_core[k].wait_recv()
        fwd_x[k].wait_recv()
        if k > 0:
            fwd_y[k - 1].wait_recv()

    for load in loads:
        load.wait()
    keep = [(1 - skip_ref[0, b]).astype(jnp.float32) for b in range(2)]
    in_gain = [in_gain_ref[b : b + 1, :] for b in range(2)]
    in_shift = [in_shift_ref[b : b + 1, :] for b in range(2)]
    mid_gain = [mid_gain_ref[b : b + 1, :] for b in range(2)]
    mid_offset = [mid_offset_ref[b : b + 1, :] for b in range(2)]

    def conv_full(k):
        return wbuf[k].reshape(channels, hidden)

    def point_full(b):
        return wpoint[b].reshape(hidden, channels)

    def at(r):
        return pl.ds(pl.multiple_of(r * size, size), size)

    def chunked(body):
        def step(r, carry):
            body(r)
            return carry

        lax.fori_loop(0, CHUNKS, step, 0)

    def start_block(r):
        spot = at(r)
        value = x_ref[spot, :].astype(jnp.float32) * in_gain[0] + in_shift[0]
        act0[spot, :] = gelu_only(value).astype(jnp.bfloat16)

    def start_slopes(r):
        spot = at(r)
        value = x_ref[spot, :].astype(jnp.float32) * in_gain[0] + in_shift[0]
        slope0[spot, :] = gelu_and_slope(value)[1] * in_gain[0]
        bgrad1[spot, :] = (keep[1] * og_ref[spot, :].astype(jnp.float32)).astype(jnp.bfloat16)

    chunked(start_block)

    part_base = 6 * PIECES
    cgrad_base = part_base + CHUNKS
    term_base = cgrad_base + CHUNKS

    def part_copy(r):
        return remote(part_out.at[at(r)], part_in.at[at(r)], part_base + r, x_mate)

    def cgrad_copy(r):
        return remote(cgrad_out.at[at(r)], cgrad_in.at[at(r)], cgrad_base + r, x_mate)

    after_x(0)
    after_x(1)
    ready(0)

    def make_part(r):
        spot = at(r)
        part_out[spot, :] = dot(act0[spot, :], conv_full(0)).astype(jnp.bfloat16)
        part_copy(r).start()

    chunked(make_part)
    after_x(2)
    after_x(3)
    after_x(4)
    after_y(1)
    after_z(3)
    after_z(4)
    after_y(2)
    chunked(start_slopes)
    ready(1)

    def make_own(r):
        spot = at(r)
        own_conv[spot, :] = dot(act0[spot, :], conv_full(1))

    chunked(make_own)
    ready(2)

    def middle_part(r):
        spot = at(r)
        part_copy(r).wait_recv()
        conv = own_conv[spot, :] + part_in[spot, :].astype(jnp.float32)
        gelu, mid_slope0 = gelu_and_slope(conv * mid_gain[0] + mid_offset[0])
        act_hidden0 = gelu.astype(jnp.bfloat16)
        hidden0[spot, :] = act_hidden0
        branch = dot(act_hidden0, point_full(0))
        state = (x_ref[spot, :].astype(jnp.float32) + keep[0] * branch).astype(jnp.bfloat16)
        gelu, slope1 = gelu_and_slope(state.astype(jnp.float32) * in_gain[1] + in_shift[1])
        if r == 0:
            after_y(3)
            ready(3)
        conv = dot(gelu.astype(jnp.bfloat16), conv_full(2))
        gelu, mid_slope1 = gelu_and_slope(conv * mid_gain[1] + mid_offset[1])
        hidden1[spot, :] = gelu.astype(jnp.bfloat16)
        if r == 0:
            after_y(4)
            ready(4)
        hidden_grad = contract_last(bgrad1[spot, :], point_full(1))
        conv_grad = (mid_slope1 * hidden_grad * mid_gain[1]).astype(jnp.bfloat16)
        act_grad = contract_last(conv_grad, conv_full(2))
        gradient = (
            og_ref[spot, :].astype(jnp.float32) + slope1 * act_grad * in_gain[1]
        ).astype(jnp.bfloat16)
        grad1[spot, :] = gradient
        branch_grad = (keep[0] * gradient.astype(jnp.float32)).astype(jnp.bfloat16)
        bgrad0[spot, :] = branch_grad
        hidden_grad = contract_last(branch_grad, point_full(0))
        cgrad_out[spot, :] = (mid_slope0 * hidden_grad * mid_gain[0]).astype(jnp.bfloat16)
        if r < CHUNKS - 1:
            cgrad_copy(r).start()

    share = hidden // 4
    half_cols = channels // 2

    def add_terms(r, b):
        spot = slice(r * size, (r + 1) * size)
        kept, branch = ((hidden0, bgrad0), (hidden1, bgrad1))[b]
        product = grad_rows(kept[spot, :], branch[spot, :])
        for owner in range(4):
            for col in range(2):
                block = product[
                    owner * share : (owner + 1) * share, col * half_cols : (col + 1) * half_cols
                ]
                first, second = (col, owner // 2) if b == 1 else (owner // 2, col)
                where = (b, owner % 2, first, second)
                if r > 0:
                    block = block + term[where]
                term[where] = block
                if r == CHUNKS - 1:
                    term_out[where] = block.astype(jnp.bfloat16)

    core_copy = [
        remote(term_out.at[b, 1 - core], core_in.at[b], term_base + b, core_mate)
        for b in range(2)
    ]
    ways = ((xpos, ypos, x_mate, y_mate), (ypos, xpos, y_mate, x_mate))
    one_copy = [remote(one_out.at[b], one_in.at[b], term_base + 2 + b, ways[b][2]) for b in range(2)]
    two_copy = [remote(two_out.at[b], two_in.at[b], term_base + 4 + b, ways[b][3]) for b in range(2)]
    z_base = term_base + 6
    z_copy = [
        remote(z_out.at[(zpos + j) % depth], z_in.at[j], z_base + j - 1, z_mates[j - 1])
        for j in range(1, depth)
    ]
    gather_base = z_base + depth - 1
    own_quarter = final.at[ypos, zpos]
    z_gather = [
        remote(own_quarter, own_quarter, gather_base + j - 1, z_mates[j - 1])
        for j in range(1, depth)
    ]
    y_gather = []
    for j in range(depth):
        quarter = final.at[ypos, (zpos + depth - j) % depth]
        y_gather.append(remote(quarter, quarter, gather_base + depth - 1 + j, y_mate))

    def last_part(r):
        spot = at(r)
        cgrad_copy(r).wait_recv()
        act_grad = contract_last(cgrad_out[spot, :], conv_full(1))
        act_grad = act_grad + contract_last(cgrad_in[spot, :], conv_full(0))
        gin_ref[spot, :] = (
            grad1[spot, :].astype(jnp.float32) + slope0[spot, :] * act_grad
        ).astype(jnp.bfloat16)
        gin_copy(r).start()

    def gin_copy(r):
        return local(gin_ref.at[at(r)], gin_hbm.at[at(r)], 7 + PIECES + r)

    for r in range(CHUNKS):
        middle_part(r)
        for b in (1, 0):
            add_terms(r, b)
            if r == CHUNKS - 1:
                core_copy[b].start()

    for b in (1, 0):
        first = ways[b][0]
        core_copy[b].wait_recv()
        away = term[b, core, 1 - first] + core_in[b, 1 - first].astype(jnp.float32)
        one_out[b] = away.astype(jnp.bfloat16)
        one_copy[b].start()
    last_part(0)
    for b in (1, 0):
        first, second = ways[b][:2]
        one_copy[b].wait_recv()
        away = term[b, core, first, 1 - second]
        away = away + core_in[b, first, 1 - second].astype(jnp.float32)
        away = away + one_in[b, 1 - second].astype(jnp.float32)
        two_out[b] = away.astype(jnp.bfloat16)
        two_copy[b].start()
    cgrad_copy(CHUNKS - 1).start()
    half_rows = share // 2
    for b in (1, 0):
        first, second = ways[b][:2]
        near = term[b, core, first, second] + core_in[b, first, second].astype(jnp.float32)
        near = near + one_in[b, second].astype(jnp.float32)
        two_copy[b].wait_recv()
        near = near + two_in[b].astype(jnp.float32)
        for part in range(2):
            block = near[part * half_rows : (part + 1) * half_rows, :]
            z_keep[2 * b + part] = block
            z_out[2 * b + part] = block.astype(jnp.bfloat16)
    for copy in z_copy:
        copy.start()
    last_part(1)
    total = z_keep[zpos]
    for j in range(1, depth):
        z_copy[j - 1].wait_recv()
        total = total + z_in[j].astype(jnp.float32)
    final[ypos, zpos] = total.astype(jnp.bfloat16)
    for copy in z_gather:
        copy.start()
    y_gather[0].start()

    def settle(col, which):
        block = final[col, which].astype(jnp.float32) * scale
        for q in range(depth):
            for side in range(2):

                @pl.when((which == q) & (col == side))
                def _():
                    spot = slice((q % 2) * half_rows, (q % 2 + 1) * half_rows)
                    pg_ref[spot, q // 2, side * half_cols : (side + 1) * half_cols] = block

    settle(ypos, zpos)
    for j in range(1, depth):
        z_gather[j - 1].wait_recv()
        y_gather[j].start()
    for j in range(1, depth):
        settle(ypos, (zpos + depth - j) % depth)
    for j in range(depth):
        y_gather[j].wait_recv()
        settle(1 - ypos, (zpos + depth - j) % depth)

    pg_copy = local(pg_ref, pg_hbm, 7 + PIECES + CHUNKS)
    pg_copy.start()
    sums = (core_copy, one_copy, two_copy, z_copy, z_gather, y_gather)
    for group in (to_core, to_x, to_z.values(), to_y, fwd_x, fwd_y) + sums:
        for copy in group:
            copy.wait_send()
    for r in range(CHUNKS):
        part_copy(r).wait_send()
        cgrad_copy(r).wait_send()
        gin_copy(r).wait()
    pg_copy.wait()


def settle_kernel(pg_from, gin_from, pg_to, gin_to, pg_ref, gin_ref, sem):
    ways = []
    for index, refs in enumerate(((pg_from, pg_ref, pg_to), (gin_from, gin_ref, gin_to))):
        count = refs[0].shape[0] // 4
        for part in range(4):
            source, middle, target = [ref.at[pl.ds(part * count, count)] for ref in refs]
            spot = 8 * index + 2 * part
            fetch = pltpu.make_async_copy(source, middle, sem.at[spot])
            ways.append((fetch, pltpu.make_async_copy(middle, target, sem.at[spot + 1])))
    for fetch, _ in ways:
        fetch.start()
    for fetch, store in ways:
        fetch.wait()
        store.start()
    for _, store in ways:
        store.wait()


def paired_shards(
    sequence_in,
    output_grad,
    skip_mask,
    in_gain,
    input_shift_vec,
    mid_gain,
    mid_offset,
    conv_weight,
    point_weight,
):
    rows, channels = sequence_in.shape[1:]
    hidden = conv_weight.shape[3]
    share = point_weight.shape[0]
    depth = lax.axis_size("dp") // 2
    taps = conv_weight.reshape(2, 3, 2, -1, hidden)
    taps_shape = taps.shape[2:]
    points_shape = (2, share // 2, channels)
    copies = 6 * PIECES + 2 * CHUNKS + 6 + 3 * depth
    hbm = pl.BlockSpec(memory_space=pltpu.HBM)
    smem = pl.BlockSpec(memory_space=pltpu.SMEM)
    bf16, f32 = jnp.bfloat16, jnp.float32
    quarter = (share // 2, channels // 2)
    half = (share, channels // 2)
    scratch = [
        pltpu.VMEM(in_gain.shape, f32),
        pltpu.VMEM(in_gain.shape, f32),
        pltpu.VMEM(mid_gain.shape, f32),
        pltpu.VMEM(mid_gain.shape, f32),
        pltpu.VMEM(point_weight.shape, bf16),
        pltpu.VMEM((share, 2, channels), f32),
        pltpu.VMEM((rows, channels), bf16),
        pltpu.VMEM((rows, channels), bf16),
        pltpu.VMEM((rows, channels), bf16),
        pltpu.VMEM((2,) + points_shape, bf16),
        pltpu.VMEM((3, 4) + taps_shape, bf16),
        pltpu.VMEM((2, 4) + points_shape, bf16),
        pltpu.VMEM((rows, channels), bf16),
        pltpu.VMEM((rows, channels), f32),
        pltpu.VMEM((rows, hidden), f32),
        pltpu.VMEM((rows, hidden), bf16),
        pltpu.VMEM((rows, hidden), bf16),
        pltpu.VMEM((rows, hidden), bf16),
        pltpu.VMEM((rows, hidden), bf16),
        pltpu.VMEM((rows, hidden), bf16),
        pltpu.VMEM((rows, hidden), bf16),
        pltpu.VMEM((rows, channels), bf16),
        pltpu.VMEM((rows, channels), bf16),
        pltpu.VMEM((rows, channels), bf16),
        pltpu.VMEM((2, 2, 2, 2) + half, f32),
        pltpu.VMEM((2, 2, 2, 2) + half, bf16),
        pltpu.VMEM((2, 2, 2) + half, bf16),
        pltpu.VMEM((2, 2) + half, bf16),
        pltpu.VMEM((2, 2) + half, bf16),
        pltpu.VMEM((2,) + half, bf16),
        pltpu.VMEM((2,) + half, bf16),
        pltpu.VMEM((depth,) + quarter, f32),
        pltpu.VMEM((depth,) + quarter, bf16),
        pltpu.VMEM((depth,) + quarter, bf16),
        pltpu.VMEM((2, depth) + quarter, bf16),
        pltpu.SemaphoreType.DMA((copies,)),
        pltpu.SemaphoreType.DMA((copies,)),
        pltpu.SemaphoreType.DMA((8 + PIECES + CHUNKS,)),
    ]
    sample_count = sequence_in.shape[0] * lax.axis_size("dp")
    full_length = rows * lax.axis_size("seq")
    scale = 1.0 / math.sqrt(sample_count * full_length)
    point_grad, gradient = pl.pallas_call(
        functools.partial(paired_kernel, scale),
        out_shape=(
            jax.ShapeDtypeStruct((share, 2, channels), f32),
            jax.ShapeDtypeStruct((rows, channels), bf16),
        ),
        in_specs=[hbm, hbm, smem] + [hbm] * 6,
        out_specs=(hbm, hbm),
        scratch_shapes=scratch,
        compiler_params=pltpu.CompilerParams(
            collective_id=0, has_side_effects=True, vmem_limit_bytes=62 * 2**20
        ),
    )(
        sequence_in.reshape(rows, channels),
        output_grad.reshape(rows, channels),
        skip_mask,
        in_gain,
        input_shift_vec,
        mid_gain,
        mid_offset,
        taps,
        point_weight,
    )
    point_grad, gradient = pl.pallas_call(
        settle_kernel,
        out_shape=(
            jax.ShapeDtypeStruct(point_grad.shape, f32),
            jax.ShapeDtypeStruct(gradient.shape, bf16),
        ),
        in_specs=[hbm, hbm],
        out_specs=(hbm, hbm),
        scratch_shapes=[
            pltpu.VMEM(point_grad.shape, f32),
            pltpu.VMEM(gradient.shape, bf16),
            pltpu.SemaphoreType.DMA((16,)),
        ],
        compiler_params=pltpu.CompilerParams(vmem_limit_bytes=62 * 2**20),
    )(point_grad, gradient)
    return (point_grad, gradient.reshape(sequence_in.shape))


def pairs_apply(sequence_in):
    count, positions = sequence_in.shape[:2]
    peers = lax.axis_size("seq")
    reach = (FIRST_DILATION // positions, SECOND_DILATION // positions)
    return (
        count == 1
        and peers == 4
        and lax.axis_size("dp") == 8
        and 2 * reach[0] == peers
        and reach[1] >= peers
    )


def shards(
    sequence_in,
    output_grad,
    skip_mask,
    in_gain,
    input_shift_vec,
    mid_gain,
    mid_offset,
    conv_weight,
    point_weight,
):
    if pairs_apply(sequence_in):
        return paired_shards(
            sequence_in,
            output_grad,
            skip_mask,
            in_gain,
            input_shift_vec,
            mid_gain,
            mid_offset,
            conv_weight,
            point_weight,
        )
    position_list = sequence_in.shape[1]
    channels = sequence_in.shape[2]
    point_full = lax.all_gather(point_weight, "seq", axis=0, tiled=True)
    neighbour_reach = (FIRST_DILATION // position_list, SECOND_DILATION // position_list)
    state = sequence_in.reshape(-1, channels)
    total_rows = state.shape[0]
    saved = []
    kept_weights = []
    for block_index in range(2):
        kept_flag = (1 - skip_mask[0, block_index]).astype(jnp.float32)
        normed = state.astype(jnp.float32) * in_gain[block_index] + input_shift_vec[block_index]
        activated = gelu_tanh(normed).astype(jnp.bfloat16)
        earlier, later = neighbours(
            activated.reshape(sequence_in.shape), neighbour_reach[block_index]
        )
        earlier = earlier.reshape(total_rows, channels)
        later = later.reshape(total_rows, channels)
        weight = lax.all_gather(conv_weight[block_index], "seq", axis=1, tiled=True)
        kept_weights.append(weight)
        operands = (
            state,
            earlier,
            activated,
            later,
            weight,
            mid_gain[block_index],
            mid_offset[block_index],
            point_full[:, block_index, :],
            kept_flag,
        )
        middle, hidden_act, state = forward_local(*operands)
        saved.append((normed, middle, hidden_act, kept_flag))
    gradient = output_grad.reshape(-1, channels)
    hidden_saved = [None, None]
    branch_saved = [None, None]
    for block_index in (1, 0):
        normed, middle, hidden_act, kept_flag = saved[block_index]
        projection = point_full[:, block_index, :]
        first_operands = (gradient, middle, projection, mid_gain[block_index], kept_flag)
        conv_grad, branch_grad = backward_first(*first_operands)
        hidden_saved[block_index] = hidden_act
        branch_saved[block_index] = branch_grad
        earlier, later = neighbours(
            conv_grad.reshape(sequence_in.shape[0], position_list, -1), neighbour_reach[block_index]
        )
        earlier = earlier.reshape(total_rows, -1)
        later = later.reshape(total_rows, -1)
        weight = lax.all_gather(conv_weight[block_index], "seq", axis=1, tiled=True)
        second_operands = (
            gradient,
            earlier,
            conv_grad,
            later,
            weight,
            normed,
            in_gain[block_index],
        )
        gradient = backward_second(*second_operands)
    first_term = grad_rows(hidden_saved[0], branch_saved[0])
    second_term = grad_rows(hidden_saved[1], branch_saved[1])
    shared_part = lax.psum_scatter(
        jnp.stack([first_term, second_term], axis=1), "seq", scatter_dimension=0, tiled=True
    )
    summed = lax.psum(shared_part, "dp")
    sample_count = sequence_in.shape[0] * lax.axis_size("dp")
    full_length = position_list * lax.axis_size("seq")
    point_grad = summed * (1.0 / math.sqrt(sample_count * full_length))
    return (point_grad, gradient.reshape(sequence_in.shape))


def solution(mesh):
    return jax.shard_map(
        shards,
        mesh=mesh,
        in_specs=(
            P("dp", "seq", None),
            P("dp", "seq", None),
            P("dp", None),
            P(),
            P(),
            P(),
            P(),
            P(None, None, "seq", None),
            P("seq", None, None),
        ),
        out_specs=(P("seq", None, None), P("dp", "seq", None)),
        check_vma=False,
    )
```

```python
import functools
import math

import jax
import jax.numpy as jnp
from jax import lax
from jax.experimental import pallas as pl
from jax.experimental.pallas import tpu as pltpu
from jax.sharding import PartitionSpec as P

FIRST_DILATION = 1024
SECOND_DILATION = 2048


def passed_along(value, axis, by):
    peers = lax.axis_size(axis)
    pairs = [(i, i + by) for i in range(peers) if 0 <= i + by < peers]
    return lax.ppermute(value, axis, pairs)


def gelu_tanh(values):
    return jax.nn.gelu(values, approximate=True)


def contract_last(left, right):
    return lax.dot_general(
        left, right, (((1,), (1,)), ((), ())), preferred_element_type=jnp.float32
    )


def neighbours(source, shards_away):
    if shards_away >= lax.axis_size("seq"):
        return (jnp.zeros_like(source), jnp.zeros_like(source))
    earlier = passed_along(source, "seq", shards_away)
    later = passed_along(source, "seq", -shards_away)
    return (earlier, later)


def forward_local(
    state, earlier, activated, later, weight, gain_vec, offset_vec, projection, kept_flag
):
    conv_out = jnp.dot(earlier, weight[0], preferred_element_type=jnp.float32)
    conv_out = conv_out + jnp.dot(activated, weight[1], preferred_element_type=jnp.float32)
    conv_out = conv_out + jnp.dot(later, weight[2], preferred_element_type=jnp.float32)
    middle = conv_out * gain_vec + offset_vec
    hidden_act = gelu_tanh(middle).astype(jnp.bfloat16)
    branch = jnp.dot(hidden_act, projection, preferred_element_type=jnp.float32)
    result = (state.astype(jnp.float32) + kept_flag * branch).astype(jnp.bfloat16)
    return (middle, hidden_act, result)


def backward_first(gradient, middle, projection, gain_vec, kept_flag):
    branch_grad = (kept_flag * gradient.astype(jnp.float32)).astype(jnp.bfloat16)
    hidden_grad = contract_last(branch_grad, projection)
    middle_grad = jax.vjp(gelu_tanh, middle)[1](hidden_grad)[0]
    conv_grad = (middle_grad * gain_vec).astype(jnp.bfloat16)
    return (conv_grad, branch_grad)


def backward_second(gradient, earlier, conv_grad, later, weight, normed, gain_vec):
    act_grad = (
        contract_last(later, weight[0])
        + contract_last(conv_grad, weight[1])
        + contract_last(earlier, weight[2])
    )
    normed_grad = jax.vjp(gelu_tanh, normed)[1](act_grad)[0] * gain_vec
    return (gradient.astype(jnp.float32) + normed_grad).astype(jnp.bfloat16)


def grad_rows(hidden_act, branch_grad):
    return lax.dot_general(
        hidden_act, branch_grad, (((0,), (0,)), ((), ())), preferred_element_type=jnp.float32
    )


MESH = pl.DeviceIdType.MESH
CHUNKS = 2
PIECES = 5
THROUGH_Z = (3, 4)
TANH_SCALE = 0.7978845608028654
CUBIC = 0.044715


def gelu_and_slope(values):
    squared = values * values
    tanh = jnp.tanh(values * (TANH_SCALE + (TANH_SCALE * CUBIC) * squared))
    gate = 0.5 + 0.5 * tanh
    bend = values * (0.5 - 0.5 * tanh * tanh)
    slope = gate + bend * (TANH_SCALE + (3.0 * TANH_SCALE * CUBIC) * squared)
    return values * gate, slope


def gelu_only(values):
    tanh = jnp.tanh(values * (TANH_SCALE + (TANH_SCALE * CUBIC) * (values * values)))
    return values * (0.5 + 0.5 * tanh)


def dot(left, right):
    return jnp.dot(left, right, preferred_element_type=jnp.float32)


def paired_kernel(
    x_hbm,
    og_hbm,
    skip_ref,
    in_gain_hbm,
    in_shift_hbm,
    mid_gain_hbm,
    mid_offset_hbm,
    cw_ref,
    pw_hbm,
    pg_hbm,
    gin_hbm,
    in_gain_ref,
    in_shift_ref,
    mid_gain_ref,
    mid_offset_ref,
    pw_ref,
    gin_ref,
    x_ref,
    og_ref,
    points,
    wbuf,
    wpoint,
    act0,
    slope0,
    own_conv,
    part_out,
    part_in,
    cgrad_out,
    cgrad_in,
    hidden0,
    hidden1,
    bgrad0,
    bgrad1,
    grad1,
    term,
    term_out,
    core_in,
    one_out,
    one_in,
    two_out,
    two_in,
    z_keep,
    z_out,
    z_in,
    final,
    ssem,
    rsem,
    lsem,
):
    seq = lax.axis_index("seq")
    dp = lax.axis_index("dp")
    core = seq % 2
    xpos = seq // 2
    ypos = dp % 2
    zpos = dp // 2
    depth = z_in.shape[0]
    core_mate = {"seq": seq + 1 - 2 * core}
    x_mate = {"seq": (seq + 2) % 4}
    y_mate = {"dp": dp + 1 - 2 * ypos}
    z_mates = [{"dp": (dp + 2 * j) % (2 * depth)} for j in range(1, depth)]
    rows = x_ref.shape[0]
    size = rows // CHUNKS
    channels = x_ref.shape[1]
    hidden = own_conv.shape[1]
    tap = 2 * xpos

    barrier = pltpu.get_barrier_semaphore()
    peers = [core_mate, x_mate, y_mate] + z_mates
    for peer in peers:
        pl.semaphore_signal(barrier, inc=1, device_id=peer, device_id_type=MESH)

    def local(src, dst, index):
        return pltpu.make_async_copy(src, dst, lsem.at[index])

    load_points = local(pw_hbm, pw_ref, 0)
    loads = [
        local(x_hbm, x_ref, 1),
        local(og_hbm, og_ref, 2),
        local(in_gain_hbm, in_gain_ref, 3),
        local(in_shift_hbm, in_shift_ref, 4),
        local(mid_gain_hbm, mid_gain_ref, 5),
        local(mid_offset_hbm, mid_offset_ref, 6),
    ]
    load_points.start()
    for load in loads:
        load.start()
    pl.semaphore_wait(barrier, len(peers))

    def remote(src, dst, index, peer):
        return pltpu.make_async_remote_copy(
            src_ref=src,
            dst_ref=dst,
            send_sem=ssem.at[index],
            recv_sem=rsem.at[index],
            device_id=peer,
            device_id_type=MESH,
        )

    def mine(piece, for_mate):
        if piece == 0:
            return cw_ref.at[0, 2 - tap if for_mate else tap]
        return (None, cw_ref.at[0, 1], points.at[0], cw_ref.at[1, 1], points.at[1])[piece]

    def place(piece, owner):
        where = (wbuf.at[0], wbuf.at[1], wpoint.at[0], wbuf.at[2], wpoint.at[1])[piece]
        return where.at[owner]

    far = (seq + 2) % 4
    zlow = zpos % 2
    z_near = {"dp": dp + 2 - 4 * zlow}

    def quarter_of(half, which):
        if half.shape[1] == hidden:
            count = half.shape[0] // 2
            return half.at[pl.ds(pl.multiple_of(which * count, count), count)]
        count = half.shape[1] // 2
        return half.at[:, pl.ds(pl.multiple_of(which * count, count), count)]

    to_core, to_x, to_y, fwd_x, fwd_y = [], [], [], [], []
    to_z = {}
    for k in range(PIECES):
        to_core.append(remote(mine(k, False), place(k, seq), 6 * k, core_mate))
        if k == 0:
            to_x.append(remote(mine(k, True), place(k, seq), 1, x_mate))
            fwd_x.append(remote(place(k, far), place(k, far), 3, core_mate))
            continue
        half = place(k, far).at[ypos]
        mine_half, there = mine(k, True).at[ypos], place(k, seq).at[ypos]
        if k in THROUGH_Z:
            mine_half, there = quarter_of(mine_half, zlow), quarter_of(there, zlow)
            quarter = quarter_of(half, zlow)
            to_z[k] = remote(quarter, quarter, 6 * k + 5, z_near)
        to_x.append(remote(mine_half, there, 6 * k + 1, x_mate))
        to_y.append(remote(half, half, 6 * k + 2, y_mate))
        fwd_x.append(remote(half, half, 6 * k + 3, core_mate))
        other = place(k, far).at[1 - ypos]
        fwd_y.append(remote(other, other, 6 * k + 4, core_mate))
    own = [local(mine(k, False), place(k, seq), 7 + k) for k in range(PIECES)]

    def send_piece(k):
        to_x[k].start()
        to_core[k].start()
        own[k].start()

    send_piece(0)
    send_piece(1)
    load_points.wait()
    for b in range(2):
        points[b] = pw_ref[:, b, :].reshape(points.shape[1:])
    for k in range(2, PIECES):
        send_piece(k)

    def after_x(k):
        to_x[k].wait_recv()
        if k in THROUGH_Z:
            to_z[k].start()
            return
        fwd_x[k].start()
        if k > 0:
            to_y[k - 1].start()

    def after_z(k):
        to_z[k].wait_recv()
        to_y[k - 1].start()
        fwd_x[k].start()

    def after_y(k):
        to_y[k - 1].wait_recv()
        fwd_y[k - 1].start()

    def ready(k):
        own[k].wait()
        to_core[k].wait_recv()
        fwd_x[k].wait_recv()
        if k > 0:
            fwd_y[k - 1].wait_recv()

    for load in loads:
        load.wait()
    keep = [(1 - skip_ref[0, b]).astype(jnp.float32) for b in range(2)]
    in_gain = [in_gain_ref[b : b + 1, :] for b in range(2)]
    in_shift = [in_shift_ref[b : b + 1, :] for b in range(2)]
    mid_gain = [mid_gain_ref[b : b + 1, :] for b in range(2)]
    mid_offset = [mid_offset_ref[b : b + 1, :] for b in range(2)]

    def conv_full(k):
        return wbuf[k].reshape(channels, hidden)

    def point_full(b):
        return wpoint[b].reshape(hidden, channels)

    def at(r):
        return pl.ds(pl.multiple_of(r * size, size), size)

    def chunked(body):
        def step(r, carry):
            body(r)
            return carry

        lax.fori_loop(0, CHUNKS, step, 0)

    def start_block(r):
        spot = at(r)
        value = x_ref[spot, :].astype(jnp.float32) * in_gain[0] + in_shift[0]
        act0[spot, :] = gelu_only(value).astype(jnp.bfloat16)

    def start_slopes(r):
        spot = at(r)
        value = x_ref[spot, :].astype(jnp.float32) * in_gain[0] + in_shift[0]
        slope0[spot, :] = gelu_and_slope(value)[1] * in_gain[0]
        bgrad1[spot, :] = (keep[1] * og_ref[spot, :].astype(jnp.float32)).astype(jnp.bfloat16)

    chunked(start_block)

    part_base = 6 * PIECES
    cgrad_base = part_base + CHUNKS
    term_base = cgrad_base + CHUNKS

    def part_copy(r):
        return remote(part_out.at[at(r)], part_in.at[at(r)], part_base + r, x_mate)

    def cgrad_copy(r):
        return remote(cgrad_out.at[at(r)], cgrad_in.at[at(r)], cgrad_base + r, x_mate)

    after_x(0)
    after_x(1)
    ready(0)

    def make_part(r):
        spot = at(r)
        part_out[spot, :] = dot(act0[spot, :], conv_full(0)).astype(jnp.bfloat16)
        part_copy(r).start()

    chunked(make_part)
    after_x(2)
    after_x(3)
    after_x(4)
    after_y(1)
    after_z(3)
    after_z(4)
    after_y(2)
    chunked(start_slopes)
    ready(1)

    def make_own(r):
        spot = at(r)
        own_conv[spot, :] = dot(act0[spot, :], conv_full(1))

    chunked(make_own)
    ready(2)

    def middle_part(r):
        spot = at(r)
        part_copy(r).wait_recv()
        conv = own_conv[spot, :] + part_in[spot, :].astype(jnp.float32)
        gelu, mid_slope0 = gelu_and_slope(conv * mid_gain[0] + mid_offset[0])
        act_hidden0 = gelu.astype(jnp.bfloat16)
        hidden0[spot, :] = act_hidden0
        branch = dot(act_hidden0, point_full(0))
        state = (x_ref[spot, :].astype(jnp.float32) + keep[0] * branch).astype(jnp.bfloat16)
        gelu, slope1 = gelu_and_slope(state.astype(jnp.float32) * in_gain[1] + in_shift[1])
        if r == 0:
            after_y(3)
            ready(3)
        conv = dot(gelu.astype(jnp.bfloat16), conv_full(2))
        gelu, mid_slope1 = gelu_and_slope(conv * mid_gain[1] + mid_offset[1])
        hidden1[spot, :] = gelu.astype(jnp.bfloat16)
        if r == 0:
            after_y(4)
            ready(4)
        hidden_grad = contract_last(bgrad1[spot, :], point_full(1))
        conv_grad = (mid_slope1 * hidden_grad * mid_gain[1]).astype(jnp.bfloat16)
        act_grad = contract_last(conv_grad, conv_full(2))
        gradient = (
            og_ref[spot, :].astype(jnp.float32) + slope1 * act_grad * in_gain[1]
        ).astype(jnp.bfloat16)
        grad1[spot, :] = gradient
        branch_grad = (keep[0] * gradient.astype(jnp.float32)).astype(jnp.bfloat16)
        bgrad0[spot, :] = branch_grad
        hidden_grad = contract_last(branch_grad, point_full(0))
        cgrad_out[spot, :] = (mid_slope0 * hidden_grad * mid_gain[0]).astype(jnp.bfloat16)
        if r < CHUNKS - 1:
            cgrad_copy(r).start()

    share = hidden // 4
    half_cols = channels // 2

    def add_terms(r, b):
        spot = slice(r * size, (r + 1) * size)
        kept, branch = ((hidden0, bgrad0), (hidden1, bgrad1))[b]
        product = grad_rows(kept[spot, :], branch[spot, :])
        for owner in range(4):
            for col in range(2):
                block = product[
                    owner * share : (owner + 1) * share, col * half_cols : (col + 1) * half_cols
                ]
                first, second = (col, owner // 2) if b == 1 else (owner // 2, col)
                where = (b, owner % 2, first, second)
                if r > 0:
                    block = block + term[where]
                term[where] = block
                if r == CHUNKS - 1:
                    term_out[where] = block.astype(jnp.bfloat16)

    core_copy = [
        remote(term_out.at[b, 1 - core], core_in.at[b], term_base + b, core_mate)
        for b in range(2)
    ]
    ways = ((xpos, ypos, x_mate, y_mate), (ypos, xpos, y_mate, x_mate))
    one_copy = [remote(one_out.at[b], one_in.at[b], term_base + 2 + b, ways[b][2]) for b in range(2)]
    two_copy = [remote(two_out.at[b], two_in.at[b], term_base + 4 + b, ways[b][3]) for b in range(2)]
    z_base = term_base + 6
    z_copy = [
        remote(z_out.at[(zpos + j) % depth], z_in.at[j], z_base + j - 1, z_mates[j - 1])
        for j in range(1, depth)
    ]
    gather_base = z_base + depth - 1
    own_quarter = final.at[ypos, zpos]
    z_gather = [
        remote(own_quarter, own_quarter, gather_base + j - 1, z_mates[j - 1])
        for j in range(1, depth)
    ]
    y_gather = []
    for j in range(depth):
        quarter = final.at[ypos, (zpos + depth - j) % depth]
        y_gather.append(remote(quarter, quarter, gather_base + depth - 1 + j, y_mate))

    def last_part(r):
        spot = at(r)
        cgrad_copy(r).wait_recv()
        act_grad = contract_last(cgrad_out[spot, :], conv_full(1))
        act_grad = act_grad + contract_last(cgrad_in[spot, :], conv_full(0))
        gin_ref[spot, :] = (
            grad1[spot, :].astype(jnp.float32) + slope0[spot, :] * act_grad
        ).astype(jnp.bfloat16)
        gin_copy(r).start()

    def gin_copy(r):
        return local(gin_ref.at[at(r)], gin_hbm.at[at(r)], 7 + PIECES + r)

    for r in range(CHUNKS):
        middle_part(r)
        for b in (1, 0):
            add_terms(r, b)
            if r == CHUNKS - 1:
                core_copy[b].start()

    for b in (1, 0):
        first = ways[b][0]
        core_copy[b].wait_recv()
        away = term[b, core, 1 - first] + core_in[b, 1 - first].astype(jnp.float32)
        one_out[b] = away.astype(jnp.bfloat16)
        one_copy[b].start()
    last_part(0)
    for b in (1, 0):
        first, second = ways[b][:2]
        one_copy[b].wait_recv()
        away = term[b, core, first, 1 - second]
        away = away + core_in[b, first, 1 - second].astype(jnp.float32)
        away = away + one_in[b, 1 - second].astype(jnp.float32)
        two_out[b] = away.astype(jnp.bfloat16)
        two_copy[b].start()
    cgrad_copy(CHUNKS - 1).start()
    half_rows = share // 2
    for b in (1, 0):
        first, second = ways[b][:2]
        near = term[b, core, first, second] + core_in[b, first, second].astype(jnp.float32)
        near = near + one_in[b, second].astype(jnp.float32)
        two_copy[b].wait_recv()
        near = near + two_in[b].astype(jnp.float32)
        for part in range(2):
            block = near[part * half_rows : (part + 1) * half_rows, :]
            z_keep[2 * b + part] = block
            z_out[2 * b + part] = block.astype(jnp.bfloat16)
    for copy in z_copy:
        copy.start()
    total = z_keep[zpos]
    for j in range(1, depth):
        z_copy[j - 1].wait_recv()
        total = total + z_in[j].astype(jnp.float32)
    final[ypos, zpos] = total.astype(jnp.bfloat16)
    for copy in z_gather:
        copy.start()
    y_gather[0].start()

    def store_piece(col, which, index):
        copy = local(final.at[col, which], pg_hbm.at[col, which], 7 + PIECES + CHUNKS + index)
        copy.start()
        return copy

    last_part(1)
    stored = [store_piece(ypos, zpos, 0)]
    for j in range(1, depth):
        z_gather[j - 1].wait_recv()
        y_gather[j].start()
    for j in range(1, depth):
        stored.append(store_piece(ypos, (zpos + depth - j) % depth, j))
    for j in range(depth):
        y_gather[j].wait_recv()
        stored.append(store_piece(1 - ypos, (zpos + depth - j) % depth, depth + j))

    sums = (core_copy, one_copy, two_copy, z_copy, z_gather, y_gather)
    for group in (to_core, to_x, to_z.values(), to_y, fwd_x, fwd_y) + sums:
        for copy in group:
            copy.wait_send()
    for r in range(CHUNKS):
        part_copy(r).wait_send()
        cgrad_copy(r).wait_send()
        gin_copy(r).wait()
    for copy in stored:
        copy.wait()


def settle_kernel(scale, sum_from, gin_from, pg_to, gin_to, sum_ref, pg_ref, gin_ref, sem):
    fetch_sum = pltpu.make_async_copy(sum_from, sum_ref, sem.at[0])
    fetch_sum.start()
    count = gin_from.shape[0] // 4
    ways = []
    for part in range(4):
        source, middle, target = [
            ref.at[pl.ds(part * count, count)] for ref in (gin_from, gin_ref, gin_to)
        ]
        fetch = pltpu.make_async_copy(source, middle, sem.at[1 + part])
        fetch.start()
        ways.append((fetch, pltpu.make_async_copy(middle, target, sem.at[5 + part])))
    fetch_sum.wait()
    rows, cols = sum_ref.shape[2:]
    stores = []
    for part in range(2):
        for b in range(2):
            for col in range(2):
                block = sum_ref[col, 2 * b + part].astype(jnp.float32) * scale
                spot = slice(part * rows, (part + 1) * rows)
                pg_ref[spot, b, col * cols : (col + 1) * cols] = block
        spot = pl.ds(part * rows, rows)
        stores.append(pltpu.make_async_copy(pg_ref.at[spot], pg_to.at[spot], sem.at[9 + part]))
        stores[-1].start()
    for fetch, store in ways:
        fetch.wait()
        store.start()
        stores.append(store)
    for store in stores:
        store.wait()


def paired_shards(
    sequence_in,
    output_grad,
    skip_mask,
    in_gain,
    input_shift_vec,
    mid_gain,
    mid_offset,
    conv_weight,
    point_weight,
):
    rows, channels = sequence_in.shape[1:]
    hidden = conv_weight.shape[3]
    share = point_weight.shape[0]
    depth = lax.axis_size("dp") // 2
    taps = conv_weight.reshape(2, 3, 2, -1, hidden)
    taps_shape = taps.shape[2:]
    points_shape = (2, share // 2, channels)
    copies = 6 * PIECES + 2 * CHUNKS + 6 + 3 * depth
    hbm = pl.BlockSpec(memory_space=pltpu.HBM)
    smem = pl.BlockSpec(memory_space=pltpu.SMEM)
    bf16, f32 = jnp.bfloat16, jnp.float32
    quarter = (share // 2, channels // 2)
    half = (share, channels // 2)
    scratch = [
        pltpu.VMEM(in_gain.shape, f32),
        pltpu.VMEM(in_gain.shape, f32),
        pltpu.VMEM(mid_gain.shape, f32),
        pltpu.VMEM(mid_gain.shape, f32),
        pltpu.VMEM(point_weight.shape, bf16),
        pltpu.VMEM((rows, channels), bf16),
        pltpu.VMEM((rows, channels), bf16),
        pltpu.VMEM((rows, channels), bf16),
        pltpu.VMEM((2,) + points_shape, bf16),
        pltpu.VMEM((3, 4) + taps_shape, bf16),
        pltpu.VMEM((2, 4) + points_shape, bf16),
        pltpu.VMEM((rows, channels), bf16),
        pltpu.VMEM((rows, channels), f32),
        pltpu.VMEM((rows, hidden), f32),
        pltpu.VMEM((rows, hidden), bf16),
        pltpu.VMEM((rows, hidden), bf16),
        pltpu.VMEM((rows, hidden), bf16),
        pltpu.VMEM((rows, hidden), bf16),
        pltpu.VMEM((rows, hidden), bf16),
        pltpu.VMEM((rows, hidden), bf16),
        pltpu.VMEM((rows, channels), bf16),
        pltpu.VMEM((rows, channels), bf16),
        pltpu.VMEM((rows, channels), bf16),
        pltpu.VMEM((2, 2, 2, 2) + half, f32),
        pltpu.VMEM((2, 2, 2, 2) + half, bf16),
        pltpu.VMEM((2, 2, 2) + half, bf16),
        pltpu.VMEM((2, 2) + half, bf16),
        pltpu.VMEM((2, 2) + half, bf16),
        pltpu.VMEM((2,) + half, bf16),
        pltpu.VMEM((2,) + half, bf16),
        pltpu.VMEM((depth,) + quarter, f32),
        pltpu.VMEM((depth,) + quarter, bf16),
        pltpu.VMEM((depth,) + quarter, bf16),
        pltpu.VMEM((2, depth) + quarter, bf16),
        pltpu.SemaphoreType.DMA((copies,)),
        pltpu.SemaphoreType.DMA((copies,)),
        pltpu.SemaphoreType.DMA((7 + PIECES + CHUNKS + 2 * depth,)),
    ]
    sample_count = sequence_in.shape[0] * lax.axis_size("dp")
    full_length = rows * lax.axis_size("seq")
    scale = 1.0 / math.sqrt(sample_count * full_length)
    summed, gradient = pl.pallas_call(
        paired_kernel,
        out_shape=(
            jax.ShapeDtypeStruct((2, depth) + quarter, bf16),
            jax.ShapeDtypeStruct((rows, channels), bf16),
        ),
        in_specs=[hbm, hbm, smem] + [hbm] * 6,
        out_specs=(hbm, hbm),
        scratch_shapes=scratch,
        compiler_params=pltpu.CompilerParams(
            collective_id=0, has_side_effects=True, vmem_limit_bytes=62 * 2**20
        ),
    )(
        sequence_in.reshape(rows, channels),
        output_grad.reshape(rows, channels),
        skip_mask,
        in_gain,
        input_shift_vec,
        mid_gain,
        mid_offset,
        taps,
        point_weight,
    )
    point_grad, gradient = pl.pallas_call(
        functools.partial(settle_kernel, scale),
        out_shape=(
            jax.ShapeDtypeStruct((share, 2, channels), f32),
            jax.ShapeDtypeStruct(gradient.shape, bf16),
        ),
        in_specs=[hbm, hbm],
        out_specs=(hbm, hbm),
        scratch_shapes=[
            pltpu.VMEM(summed.shape, bf16),
            pltpu.VMEM((share, 2, channels), f32),
            pltpu.VMEM(gradient.shape, bf16),
            pltpu.SemaphoreType.DMA((11,)),
        ],
        compiler_params=pltpu.CompilerParams(vmem_limit_bytes=62 * 2**20),
    )(summed, gradient)
    return (point_grad, gradient.reshape(sequence_in.shape))


def pairs_apply(sequence_in):
    count, positions = sequence_in.shape[:2]
    peers = lax.axis_size("seq")
    reach = (FIRST_DILATION // positions, SECOND_DILATION // positions)
    return (
        count == 1
        and peers == 4
        and lax.axis_size("dp") == 8
        and 2 * reach[0] == peers
        and reach[1] >= peers
    )


def shards(
    sequence_in,
    output_grad,
    skip_mask,
    in_gain,
    input_shift_vec,
    mid_gain,
    mid_offset,
    conv_weight,
    point_weight,
):
    if pairs_apply(sequence_in):
        return paired_shards(
            sequence_in,
            output_grad,
            skip_mask,
            in_gain,
            input_shift_vec,
            mid_gain,
            mid_offset,
            conv_weight,
            point_weight,
        )
    position_list = sequence_in.shape[1]
    channels = sequence_in.shape[2]
    point_full = lax.all_gather(point_weight, "seq", axis=0, tiled=True)
    neighbour_reach = (FIRST_DILATION // position_list, SECOND_DILATION // position_list)
    state = sequence_in.reshape(-1, channels)
    total_rows = state.shape[0]
    saved = []
    kept_weights = []
    for block_index in range(2):
        kept_flag = (1 - skip_mask[0, block_index]).astype(jnp.float32)
        normed = state.astype(jnp.float32) * in_gain[block_index] + input_shift_vec[block_index]
        activated = gelu_tanh(normed).astype(jnp.bfloat16)
        earlier, later = neighbours(
            activated.reshape(sequence_in.shape), neighbour_reach[block_index]
        )
        earlier = earlier.reshape(total_rows, channels)
        later = later.reshape(total_rows, channels)
        weight = lax.all_gather(conv_weight[block_index], "seq", axis=1, tiled=True)
        kept_weights.append(weight)
        operands = (
            state,
            earlier,
            activated,
            later,
            weight,
            mid_gain[block_index],
            mid_offset[block_index],
            point_full[:, block_index, :],
            kept_flag,
        )
        middle, hidden_act, state = forward_local(*operands)
        saved.append((normed, middle, hidden_act, kept_flag))
    gradient = output_grad.reshape(-1, channels)
    hidden_saved = [None, None]
    branch_saved = [None, None]
    for block_index in (1, 0):
        normed, middle, hidden_act, kept_flag = saved[block_index]
        projection = point_full[:, block_index, :]
        first_operands = (gradient, middle, projection, mid_gain[block_index], kept_flag)
        conv_grad, branch_grad = backward_first(*first_operands)
        hidden_saved[block_index] = hidden_act
        branch_saved[block_index] = branch_grad
        earlier, later = neighbours(
            conv_grad.reshape(sequence_in.shape[0], position_list, -1), neighbour_reach[block_index]
        )
        earlier = earlier.reshape(total_rows, -1)
        later = later.reshape(total_rows, -1)
        weight = lax.all_gather(conv_weight[block_index], "seq", axis=1, tiled=True)
        second_operands = (
            gradient,
            earlier,
            conv_grad,
            later,
            weight,
            normed,
            in_gain[block_index],
        )
        gradient = backward_second(*second_operands)
    first_term = grad_rows(hidden_saved[0], branch_saved[0])
    second_term = grad_rows(hidden_saved[1], branch_saved[1])
    shared_part = lax.psum_scatter(
        jnp.stack([first_term, second_term], axis=1), "seq", scatter_dimension=0, tiled=True
    )
    summed = lax.psum(shared_part, "dp")
    sample_count = sequence_in.shape[0] * lax.axis_size("dp")
    full_length = position_list * lax.axis_size("seq")
    point_grad = summed * (1.0 / math.sqrt(sample_count * full_length))
    return (point_grad, gradient.reshape(sequence_in.shape))


def solution(mesh):
    return jax.shard_map(
        shards,
        mesh=mesh,
        in_specs=(
            P("dp", "seq", None),
            P("dp", "seq", None),
            P("dp", None),
            P(),
            P(),
            P(),
            P(),
            P(None, None, "seq", None),
            P("seq", None, None),
        ),
        out_specs=(P("seq", None, None), P("dp", "seq", None)),
        check_vma=False,
    )
```
